32 devices in a mesh: blk: 2 (over y), grp: 16 (over z, x, core).
Axes of the slice: x: 2, y: 2, z: 4, core: 2. Of those that a mesh axis runs over, the one named last changes fastest.
Arguments:
- inputs: float32 [8, 4096], P(None, ('blk', 'grp')), may hold values from 0 to 1
- probes: float32 [16, 4096], P(None, ('blk', 'grp')), may hold values from -2 to 2
- lengths: float32 [8], replicated, may hold values from 0.2 to 0.6
- noise: float32 [1], replicated, may hold values from 0.1 to 1
- pivots: int32 [128], replicated, may hold values from 0 to 4095, as said below
Outputs:
- panel: float32 [128, 4096], P(None, ('blk', 'grp'))
- product: float32 [16, 4096], P(None, ('blk', 'grp'))
The draws below stay inside these ranges and needn't reach their ends.
Inputs may be any that keep to these rules, and one draw needn't show every extreme that they name: `pivots`: the indices are distinct.
All inputs are finite; a program needn't handle non-finite values.
Results may differ from the reference program's by a relative error of at most 0.00027.
Values sent between devices are 32-bit elements; how exact they have to be, the bound alone decides.
No kernel may reach another device: no remote copies, remote signals or barrier semaphores. Data moves between devices by JAX's collectives and lax.ppermute only.
A program may use at most 64 MiB of HBM per device.

```python
import math
import jax
import jax.numpy as jnp
from jax import lax

D = 8
PROBES = 16
PIV = 128
N = 4096


def draw_pivots(key, part):
    middle = 1 + jax.random.permutation(jax.random.fold_in(key, 3), N - 2)[:PIV - 2]
    values = jnp.concatenate([jnp.zeros((1,), jnp.int32), middle.astype(jnp.int32), jnp.full((1,), N - 1, jnp.int32)])
    return jax.random.permutation(jax.random.fold_in(key, 5), values).astype(jnp.int32)


def level_of(rng, dims, shards, least, high):
    factor_of, own = 1.0, jax.random.fold_in(rng, 6)
    for position, blocks in shards:
        draws = jnp.exp(jax.random.uniform(jax.random.fold_in(own, position), (blocks,), jnp.float32, least / len(shards), high / len(shards)))
        factor_of = factor_of * jnp.repeat(draws, dims[position] // blocks).reshape([-1 if axis == position else 1 for axis in range(len(dims))])
    return factor_of


def bell_draw(own_key, shape, deviation, reach, split=(), kind=jnp.bfloat16):
    values = deviation * jax.random.normal(own_key, shape, jnp.float32)
    if split:
        values = values * level_of(own_key, shape, split, -0.22, 0.18)
    return jnp.clip(values, -reach, reach).astype(kind)


def setup_inputs(seed: int = 0) -> dict:
    splits = jax.random.split(jax.random.key(seed), 6)
    return {
        "inputs": jnp.clip(1.0 * jax.random.uniform(splits[0], (D, N), jnp.float32) ** level_of(splits[0], (D, N), ((1, 32),), -0.2, 0.2), 0.0, 1.0),
        "probes": bell_draw(splits[1], (PROBES, N), 0.3, 2.0, ((1, 32),), jnp.float32),
        "lengths": jnp.clip(jnp.exp(jax.random.uniform(splits[2], (D,), jnp.float32, math.log(0.2), math.log(0.6))), 0.2, 0.6),
        "noise": jnp.clip(jnp.exp(jax.random.uniform(splits[3], (1,), jnp.float32, math.log(0.1), math.log(1.0))), 0.1, 1.0),
        "pivots": draw_pivots(jax.random.fold_in(splits[5], 71), 0),
    }


def kernel(left, right):
    cross = jnp.dot(left.T.astype(jnp.float32), right.astype(jnp.float32), precision=lax.Precision.HIGHEST, preferred_element_type=jnp.float32)
    dist = lax.optimization_barrier(jnp.sum(left * left, 0))[:, None] + lax.optimization_barrier(jnp.sum(right * right, 0))[None, :] - 2.0 * cross
    radius = jnp.sqrt(5.0 * jnp.maximum(dist, 0.0))
    return (1.0 + radius + radius * radius / 3.0) * jnp.exp(-radius)

def reference(inputs, probes, lengths, noise, pivots):
    scaled = inputs / lengths[:, None]
    pivot_x = jnp.take(scaled, pivots.astype(jnp.int32), axis=1)
    count = pivot_x.shape[1]
    inner = kernel(pivot_x, pivot_x) + noise[0] * jnp.eye(count, dtype=jnp.float32)
    lower = jnp.linalg.cholesky(inner)
    panel = lax.linalg.triangular_solve(lower, kernel(pivot_x, scaled), left_side=True, lower=True)
    total_pts = scaled.shape[1]
    width = math.gcd(total_pts, 2048)
    blocks = total_pts // width
    x_tiles = jnp.transpose(scaled.reshape(scaled.shape[0], blocks, width), (1, 0, 2))
    v_tiles = jnp.transpose(probes.reshape(probes.shape[0], blocks, width), (1, 0, 2))

    def row_block(rows_x):

        def col_step(acc, item):
            cols_x, cols_v = item
            part_sum = jnp.dot(cols_v.astype(jnp.float32), kernel(cols_x, rows_x).astype(jnp.float32), precision=lax.Precision.HIGHEST, preferred_element_type=jnp.float32)
            return (acc + part_sum, None)
        start = jnp.zeros((probes.shape[0], width), jnp.float32)
        acc, unused = lax.scan(col_step, start, (x_tiles, v_tiles))
        return acc
    result = lax.map(row_block, x_tiles)
    product = jnp.transpose(result, (1, 0, 2)).reshape(probes.shape[0], total_pts)
    return (panel, product + noise[0] * probes)
```

```python
import math

import jax
import jax.numpy as jnp
from jax import lax
from jax.experimental import pallas as pl
from jax.experimental.pallas import tpu as pltpu
from jax.sharding import PartitionSpec as P

F32 = jnp.float32
BF16 = jnp.bfloat16
LN2 = math.log(2.0)
SCALE = math.sqrt(5.0) / LN2
BLOCK = 16
CHUNK = 4
UNROLL = 32


def exchange_masks(groups, members):
    low = members.bit_length() - 1
    bits = [1 << bit for bit in range(low - 1, 1, -1)]
    bits += [1 << (low + bit) for bit in range(groups.bit_length() - 2, -1, -1)]
    bits += [2] if members > 2 else []
    return [bit | 1 for bit in bits] + [1]


def split3(value):
    high = value.astype(BF16).astype(F32)
    rest = value - high
    middle = rest.astype(BF16).astype(F32)
    return high, middle, rest - middle


def norm_tile(x, first):
    high, middle, low = split3(jnp.sum(x * x, axis=0, keepdims=True))
    row = lax.broadcasted_iota(jnp.int32, x.shape, 0)
    if not first:
        row = jnp.where(row < 3, row + 3, row - 3)
    tile = jnp.where(row < 6, 1.0, 0.0)
    tile = jnp.where(row == 0, high, tile)
    tile = jnp.where(row == 1, middle, tile)
    return jnp.where(row == 2, low, tile)


def left_stack(x):
    high, middle, low = split3(x)
    return jnp.concatenate(
        [high, high, high, middle, middle, low, norm_tile(x, True), jnp.zeros_like(x)], 0
    )


def right_stack(x):
    high, middle, low = split3(-2.0 * x)
    return jnp.concatenate(
        [high, middle, low, high, middle, high, norm_tile(x, False), jnp.zeros_like(x)], 0
    ).astype(BF16)


def matern(square):
    square = jnp.maximum(square, 1e-30)
    radius = square * lax.rsqrt(square)
    return (1.0 + LN2 * radius + (LN2 * LN2 / 3.0) * square) * jnp.exp2(-radius)


def rows_of(value, row):
    return jnp.broadcast_to(value[row : row + 1, :], value.shape)


def eliminate(a, b, panel_ref, step):
    tiles = BLOCK // 8
    base = step * BLOCK
    sub = lax.broadcasted_iota(jnp.int32, (8, 128), 0)
    ra = [a[8 * t : 8 * t + 8] for t in range(tiles)]
    rb = [b[8 * t : 8 * t + 8] for t in range(tiles)]
    cols = [
        [jnp.broadcast_to(ra[t][:, base + m : base + m + 1], (8, 128)) for t in range(tiles)]
        for m in range(BLOCK)
    ]
    out = [jnp.zeros((8, 128), F32) for t in range(tiles)]
    for j in range(BLOCK):
        v, s = divmod(j, 8)
        pivot = rows_of(cols[j][v], s)
        inverse = 1.0 / pivot
        out[v] = jnp.where(sub == s, rb[v] * lax.rsqrt(pivot), out[v])
        coef = list(cols[j])
        coef[v] = coef[v] - jnp.where(sub == s, 1.0, 0.0)
        row_a = rows_of(ra[v], s) * inverse
        row_b = rows_of(rb[v], s) * inverse
        for t in range(tiles):
            ra[t] = ra[t] - coef[t] * row_a
            rb[t] = rb[t] - coef[t] * row_b
        for m in range(j + 1, BLOCK):
            entry = rows_of(cols[m][v], s) * inverse
            for t in range(tiles):
                cols[m][t] = cols[m][t] - coef[t] * entry
    for t in range(tiles):
        panel_ref[base + 8 * t : base + 8 * t + 8, :] = out[t]
    if base + BLOCK == panel_ref.shape[0]:
        return None, None
    solved = jnp.concatenate(
        [jnp.concatenate(ra, 0), jnp.concatenate(rb, 0)], 1
    )
    w_high, w_middle, w_low = split3(solved)
    right = jnp.concatenate([w_high, w_middle, w_low, w_high, w_middle, w_high], 0).astype(BF16)
    l_high, l_middle, l_low = split3(a[BLOCK:, base : base + BLOCK])
    left = jnp.concatenate([l_high, l_high, l_high, l_middle, l_middle, l_low], 1).astype(BF16)
    change = jnp.dot(left, right, preferred_element_type=F32)
    return a[BLOCK:] - change[:, :128], b[BLOCK:] - change[:, 128:]


def make_body(masks, count, members):
    half = count // 2

    def owner(index):
        mask = 0
        for bit, value in enumerate(masks):
            mask = mask ^ (((index >> bit) & 1) * value)
        return mask

    def body(noise_ref, pivots_ref, own_ref, here_ref, there_ref, panel_ref, product_ref):
        me = lax.axis_index("blk") * members + lax.axis_index("grp")
        noise = noise_ref[0]
        rows = own_ref.shape[1]
        dims = own_ref.shape[0] - product_ref.shape[0]
        pivots = pivots_ref[...]
        points = lax.broadcasted_iota(jnp.int32, (rows, pivots.shape[1]), 0)

        def pick(total, ref, index, first):
            device = me ^ owner(index + first)
            hot = (points == pivots - device * rows).astype(F32).astype(BF16)
            parts = jnp.concatenate(split3(ref[index, :dims, :]), 0).astype(BF16)
            return total + jnp.dot(parts, hot, preferred_element_type=F32)

        picked = jnp.zeros((3 * dims, pivots.shape[1]), F32)
        for ref, first in ((here_ref, 0), (there_ref, half)):
            if half <= UNROLL:
                for index in range(half):
                    picked = pick(picked, ref, index, first)
            else:
                picked = lax.fori_loop(
                    0, half, lambda i, t, r=ref, f=first: pick(t, r, i, f), picked
                )
        pivot_x = picked[:dims] + picked[dims : 2 * dims] + picked[2 * dims :]
        own = own_ref[:dims, :]
        left_pivot = left_stack(pivot_x).T.astype(BF16)
        both = jnp.concatenate([right_stack(pivot_x), right_stack(own)], 1)
        values = matern(jnp.dot(left_pivot, both, preferred_element_type=F32))
        size = pivots.shape[1]
        eye = lax.broadcasted_iota(jnp.int32, (size, size), 0) == lax.broadcasted_iota(
            jnp.int32, (size, size), 1
        )
        a = values[:, :size] + jnp.where(eye, noise, 0.0)
        b = values[:, size:]
        left_own = left_stack(own).T.astype(BF16)
        nt = (((1,), (1,)), ((), ()))

        def add_chunk(carry, ref, index):
            wide, narrow = carry
            blocks = [ref[index + i] for i in range(CHUNK)]
            right = jnp.concatenate([right_stack(block[:dims]) for block in blocks], 1)
            probe = jnp.concatenate([block[dims:] for block in blocks], 1)
            probe_high = probe.astype(BF16)
            probe_low = (probe - probe_high.astype(F32)).astype(BF16)
            value = matern(jnp.dot(left_own, right, preferred_element_type=F32))
            value_high = value.astype(BF16)
            value_low = (value - value_high.astype(F32)).astype(BF16)
            wide = wide + lax.dot_general(
                value_high,
                jnp.concatenate([probe_high, probe_low], 0),
                nt,
                preferred_element_type=F32,
            )
            narrow = narrow + lax.dot_general(
                value_low, probe_high, nt, preferred_element_type=F32
            )
            return wide, narrow

        vectors = product_ref.shape[0]
        carry = (jnp.zeros((rows, 2 * vectors), F32), jnp.zeros((rows, vectors), F32))
        chunks = [(ref, i * CHUNK) for ref in (here_ref, there_ref) for i in range(half // CHUNK)]
        unrolled = half <= UNROLL
        steps = size // BLOCK
        for step in range(steps):
            a, b = eliminate(a, b, panel_ref, step)
            if unrolled:
                for ref, index in chunks[step::steps]:
                    carry = add_chunk(carry, ref, index)
        if not unrolled:
            for ref in (here_ref, there_ref):
                carry = lax.fori_loop(
                    0, half // CHUNK, lambda i, c, r=ref: add_chunk(c, r, i * CHUNK), carry
                )
        wide, narrow = carry
        total = wide[:, :vectors] + wide[:, vectors:] + narrow
        product_ref[...] = total.T + noise * own_ref[dims:, :]

    return body


def solution(mesh):
    groups, members = mesh.shape["blk"], mesh.shape["grp"]
    count = groups * members
    masks = exchange_masks(groups, members)

    def swap(value, mask):
        return lax.ppermute(value, ("blk", "grp"), [(i, i ^ mask) for i in range(count)])

    def local(inputs, probes, lengths, noise, pivots):
        rows = inputs.shape[1]
        own = jnp.concatenate([inputs * (SCALE / lengths)[:, None], probes], 0)
        here = own[None]
        for mask in masks[:-1]:
            here = jnp.concatenate([here, swap(here, mask)], 0)
        there = swap(here, masks[-1])
        vmem = pl.BlockSpec(memory_space=pltpu.VMEM)
        return pl.pallas_call(
            make_body(masks, count, members),
            out_shape=(
                jax.ShapeDtypeStruct((pivots.shape[0], rows), F32),
                jax.ShapeDtypeStruct(probes.shape, F32),
            ),
            in_specs=[pl.BlockSpec(memory_space=pltpu.SMEM)] + [vmem] * 4,
            out_specs=(vmem, vmem),
            compiler_params=pltpu.CompilerParams(vmem_limit_bytes=32 * 1024 * 1024),
        )(noise, pivots[None, :], own, here, there)

    in_specs = (P(None, ("blk", "grp")), P(None, ("blk", "grp")), P(), P(), P())
    out_specs = (P(None, ("blk", "grp")), P(None, ("blk", "grp")))
    return jax.shard_map(local, mesh=mesh, in_specs=in_specs, out_specs=out_specs, check_vma=False)
```

```python
import math

import jax
import jax.numpy as jnp
from jax import lax
from jax.experimental import pallas as pl
from jax.experimental.pallas import tpu as pltpu
from jax.sharding import PartitionSpec as P

F32 = jnp.float32
BF16 = jnp.bfloat16
LN2 = math.log(2.0)
SCALE = math.sqrt(5.0) / LN2
BLOCK = 16
CHUNK = 4
UNROLL = 32


def exchange_masks(groups, members):
    low = members.bit_length() - 1
    bits = [1 << bit for bit in range(low - 1, 1, -1)]
    bits += [1 << (low + bit) for bit in range(groups.bit_length() - 2, -1, -1)]
    bits += [2] if members > 2 else []
    even = [bit | 1 for bit in bits]
    odd = even[:-2] + even[:-3:-1]
    return even + [1], odd + [1]


def parity(index, count):
    bits = 0
    for bit in range(count.bit_length() - 1):
        bits = bits ^ (index >> bit)
    return bits & 1


def split3(value):
    high = value.astype(BF16).astype(F32)
    rest = value - high
    middle = rest.astype(BF16).astype(F32)
    return high, middle, rest - middle


def norm_tile(x, first):
    high, middle, low = split3(jnp.sum(x * x, axis=0, keepdims=True))
    row = lax.broadcasted_iota(jnp.int32, x.shape, 0)
    if not first:
        row = jnp.where(row < 3, row + 3, row - 3)
    tile = jnp.where(row < 6, 1.0, 0.0)
    tile = jnp.where(row == 0, high, tile)
    tile = jnp.where(row == 1, middle, tile)
    return jnp.where(row == 2, low, tile)


def left_stack(x):
    high, middle, low = split3(x)
    return jnp.concatenate(
        [high, high, high, middle, middle, low, norm_tile(x, True), jnp.zeros_like(x)], 0
    )


def right_stack(x):
    high, middle, low = split3(-2.0 * x)
    return jnp.concatenate(
        [high, middle, low, high, middle, high, norm_tile(x, False), jnp.zeros_like(x)], 0
    ).astype(BF16)


def matern(square):
    square = jnp.maximum(square, 1e-30)
    radius = square * lax.rsqrt(square)
    return (1.0 + LN2 * radius + (LN2 * LN2 / 3.0) * square) * jnp.exp2(-radius)


def rows_of(value, row):
    return jnp.broadcast_to(value[row : row + 1, :], value.shape)


def eliminate(a, b, panel_ref, step):
    tiles = BLOCK // 8
    base = step * BLOCK
    sub = lax.broadcasted_iota(jnp.int32, (8, 128), 0)
    ra = [a[8 * t : 8 * t + 8] for t in range(tiles)]
    rb = [b[8 * t : 8 * t + 8] for t in range(tiles)]
    cols = [
        [jnp.broadcast_to(ra[t][:, base + m : base + m + 1], (8, 128)) for t in range(tiles)]
        for m in range(BLOCK)
    ]
    out = [jnp.zeros((8, 128), F32) for t in range(tiles)]
    for j in range(BLOCK):
        v, s = divmod(j, 8)
        pivot = rows_of(cols[j][v], s)
        inverse = 1.0 / pivot
        out[v] = jnp.where(sub == s, rb[v] * lax.rsqrt(pivot), out[v])
        coef = list(cols[j])
        coef[v] = coef[v] - jnp.where(sub == s, 1.0, 0.0)
        row_a = rows_of(ra[v], s) * inverse
        row_b = rows_of(rb[v], s) * inverse
        for t in range(tiles):
            ra[t] = ra[t] - coef[t] * row_a
            rb[t] = rb[t] - coef[t] * row_b
        for m in range(j + 1, BLOCK):
            entry = rows_of(cols[m][v], s) * inverse
            for t in range(tiles):
                cols[m][t] = cols[m][t] - coef[t] * entry
    for t in range(tiles):
        panel_ref[base + 8 * t : base + 8 * t + 8, :] = out[t]
    if base + BLOCK == panel_ref.shape[0]:
        return None, None
    solved = jnp.concatenate(
        [jnp.concatenate(ra, 0), jnp.concatenate(rb, 0)], 1
    )
    w_high, w_middle, w_low = split3(solved)
    right = jnp.concatenate([w_high, w_middle, w_low, w_high, w_middle, w_high], 0).astype(BF16)
    l_high, l_middle, l_low = split3(a[BLOCK:, base : base + BLOCK])
    left = jnp.concatenate([l_high, l_high, l_high, l_middle, l_middle, l_low], 1).astype(BF16)
    change = jnp.dot(left, right, preferred_element_type=F32)
    return a[BLOCK:] - change[:, :128], b[BLOCK:] - change[:, 128:]


def make_body(masks, count, members):
    half = count // 2

    def owner(me, kind, index):
        for bit, (even, odd) in enumerate(zip(masks[0][:-1], masks[1][:-1])):
            me = me ^ (((index >> bit) & 1) * jnp.where(kind == 0, even, odd))
        return me

    def body(side_ref, own_ref, here_ref, there_ref, panel_ref, product_ref):
        me = lax.axis_index("blk") * members + lax.axis_index("grp")
        rows = own_ref.shape[1]
        dims = own_ref.shape[0] - product_ref.shape[0]
        scale = side_ref[:dims, :]
        noise = side_ref[dims : dims + 1, :]
        pivots = side_ref[dims + 1 : dims + 2, :].astype(jnp.int32)
        points = lax.broadcasted_iota(jnp.int32, (rows, pivots.shape[1]), 0)

        kind = parity(me, count)

        def pick(total, ref, index, other):
            device = owner(me ^ other, kind ^ other, index)
            hot = (points == pivots - device * rows).astype(F32).astype(BF16)
            parts = jnp.concatenate(split3(ref[index, :dims, :]), 0).astype(BF16)
            return total + jnp.dot(parts, hot, preferred_element_type=F32)

        picked = jnp.zeros((3 * dims, pivots.shape[1]), F32)
        for ref, other in ((here_ref, 0), (there_ref, 1)):
            if half <= UNROLL:
                for index in range(half):
                    picked = pick(picked, ref, index, other)
            else:
                picked = lax.fori_loop(
                    0, half, lambda i, t, r=ref, o=other: pick(t, r, i, o), picked
                )
        pivot_x = (picked[:dims] + picked[dims : 2 * dims] + picked[2 * dims :]) * scale
        own = own_ref[:dims, :] * scale
        left_pivot = left_stack(pivot_x).T.astype(BF16)
        both = jnp.concatenate([right_stack(pivot_x), right_stack(own)], 1)
        values = matern(jnp.dot(left_pivot, both, preferred_element_type=F32))
        size = pivots.shape[1]
        eye = lax.broadcasted_iota(jnp.int32, (size, size), 0) == lax.broadcasted_iota(
            jnp.int32, (size, size), 1
        )
        a = values[:, :size] + jnp.where(eye, noise, 0.0)
        b = values[:, size:]
        left_own = left_stack(own).T.astype(BF16)
        nt = (((1,), (1,)), ((), ()))

        def add_chunk(carry, ref, index):
            wide, narrow = carry
            blocks = [ref[index + i] for i in range(CHUNK)]
            right = jnp.concatenate([right_stack(block[:dims] * scale) for block in blocks], 1)
            probe = jnp.concatenate([block[dims:] for block in blocks], 1)
            probe_high = probe.astype(BF16)
            probe_low = (probe - probe_high.astype(F32)).astype(BF16)
            value = matern(jnp.dot(left_own, right, preferred_element_type=F32))
            value_high = value.astype(BF16)
            value_low = (value - value_high.astype(F32)).astype(BF16)
            wide = wide + lax.dot_general(
                value_high,
                jnp.concatenate([probe_high, probe_low], 0),
                nt,
                preferred_element_type=F32,
            )
            narrow = narrow + lax.dot_general(
                value_low, probe_high, nt, preferred_element_type=F32
            )
            return wide, narrow

        vectors = product_ref.shape[0]
        carry = (jnp.zeros((rows, 2 * vectors), F32), jnp.zeros((rows, vectors), F32))
        chunks = [(ref, i * CHUNK) for ref in (here_ref, there_ref) for i in range(half // CHUNK)]
        unrolled = half <= UNROLL
        steps = size // BLOCK
        for step in range(steps):
            a, b = eliminate(a, b, panel_ref, step)
            if unrolled:
                for ref, index in chunks[step::steps]:
                    carry = add_chunk(carry, ref, index)
        if not unrolled:
            for ref in (here_ref, there_ref):
                carry = lax.fori_loop(
                    0, half // CHUNK, lambda i, c, r=ref: add_chunk(c, r, i * CHUNK), carry
                )
        wide, narrow = carry
        total = wide[:, :vectors] + wide[:, vectors:] + narrow
        product_ref[...] = total.T + noise * own_ref[dims:, :]

    return body


def solution(mesh):
    groups, members = mesh.shape["blk"], mesh.shape["grp"]
    count = groups * members
    masks = exchange_masks(groups, members)

    def swap(value, step):
        pairs = [(i, i ^ masks[parity(i, count)][step]) for i in range(count)]
        return lax.ppermute(value, ("blk", "grp"), pairs)

    def local(inputs, probes, lengths, noise, pivots):
        rows = inputs.shape[1]
        own = jnp.concatenate([inputs, probes], 0)
        here = own[None]
        for step in range(len(masks[0]) - 1):
            if step == 1:
                side = jnp.concatenate(
                    [
                        jnp.broadcast_to((SCALE / lengths)[:, None], inputs.shape),
                        jnp.broadcast_to(noise[:, None], (1, rows)),
                        pivots.astype(F32)[None, :],
                    ],
                    0,
                )
            here = jnp.concatenate([here, swap(here, step)], 0)
        there = swap(here, len(masks[0]) - 1)
        vmem = pl.BlockSpec(memory_space=pltpu.VMEM)
        return pl.pallas_call(
            make_body(masks, count, members),
            out_shape=(
                jax.ShapeDtypeStruct((pivots.shape[0], rows), F32),
                jax.ShapeDtypeStruct(probes.shape, F32),
            ),
            in_specs=[vmem] * 4,
            out_specs=(vmem, vmem),
            compiler_params=pltpu.CompilerParams(vmem_limit_bytes=32 * 1024 * 1024),
        )(side, own, here, there)

    in_specs = (P(None, ("blk", "grp")), P(None, ("blk", "grp")), P(), P(), P())
    out_specs = (P(None, ("blk", "grp")), P(None, ("blk", "grp")))
    return jax.shard_map(local, mesh=mesh, in_specs=in_specs, out_specs=out_specs, check_vma=False)
```

```python
import functools
import math

import jax
import jax.numpy as jnp
from jax import lax
from jax.experimental import pallas as pl
from jax.experimental.pallas import tpu as pltpu
from jax.sharding import PartitionSpec as P

F32 = jnp.float32
BF16 = jnp.bfloat16
LN2 = math.log(2.0)
SCALE = math.sqrt(5.0) / LN2
BLOCK = 16
CHUNK = 4
PICK = 2
UNROLL = 32


def exchange_masks(groups, members):
    low = members.bit_length() - 1
    bits = [1 << bit for bit in range(low - 1, 1, -1)]
    bits += [1 << (low + bit) for bit in range(groups.bit_length() - 2, -1, -1)]
    bits += [2] if members > 2 else []
    even = [bit | 1 for bit in bits]
    odd = even[:-2] + even[:-3:-1]
    return even + [1], odd + [1]


def parity(index, count):
    bits = 0
    for bit in range(count.bit_length() - 1):
        bits = bits ^ (index >> bit)
    return bits & 1


def split3(value):
    high = value.astype(BF16).astype(F32)
    rest = value - high
    middle = rest.astype(BF16).astype(F32)
    return high, middle, rest - middle


def norm_tile(x, first):
    high, middle, low = split3(jnp.sum(x * x, axis=0, keepdims=True))
    row = lax.broadcasted_iota(jnp.int32, x.shape, 0)
    if not first:
        row = jnp.where(row < 3, row + 3, row - 3)
    tile = jnp.where(row < 6, 1.0, 0.0)
    tile = jnp.where(row == 0, high, tile)
    tile = jnp.where(row == 1, middle, tile)
    return jnp.where(row == 2, low, tile)


def left_stack(x):
    high, middle, low = split3(x)
    return jnp.concatenate(
        [high, high, high, middle, middle, low, norm_tile(x, True), jnp.zeros_like(x)], 0
    )


def right_stack(x):
    high, middle, low = split3(-2.0 * x)
    return jnp.concatenate(
        [high, middle, low, high, middle, high, norm_tile(x, False), jnp.zeros_like(x)], 0
    ).astype(BF16)


def matern(square):
    square = jnp.maximum(square, 1e-30)
    radius = square * lax.rsqrt(square)
    return (1.0 + LN2 * radius + (LN2 * LN2 / 3.0) * square) * jnp.exp2(-radius)


def rows_of(value, row):
    return jnp.broadcast_to(value[row : row + 1, :], value.shape)


def eliminate(a, b, step):
    tiles = BLOCK // 8
    base, first = step * BLOCK, step * tiles
    later = first + 2 * tiles
    sub = lax.broadcasted_iota(jnp.int32, (8, 128), 0)

    def column(piece, m):
        return jnp.broadcast_to(piece[:, base + m : base + m + 1], (8, 128))

    ra, rb = a[first : first + tiles], b[first : first + tiles]
    cols = [[column(piece, m) for piece in ra] for m in range(BLOCK)]
    below = [[column(piece, m) for piece in a[first + tiles : later]] for m in range(BLOCK)]
    if later < len(a):
        l_high, l_middle, l_low = split3(
            jnp.concatenate([piece[:, base : base + BLOCK] for piece in a[later:]], 0)
        )
        left = jnp.concatenate([l_high, l_high, l_high, l_middle, l_middle, l_low], 1).astype(BF16)
    out = [jnp.zeros((8, 128), F32) for t in range(tiles)]
    for j in range(BLOCK):
        v, s = divmod(j, 8)
        pivot = rows_of(cols[j][v], s)
        inverse = 1.0 / pivot
        out[v] = jnp.where(sub == s, rb[v] * lax.rsqrt(pivot), out[v])
        coef = list(cols[j])
        coef[v] = coef[v] - jnp.where(sub == s, 1.0, 0.0)
        row_a = rows_of(ra[v], s) * inverse
        row_b = rows_of(rb[v], s) * inverse
        for t in range(tiles):
            ra[t] = ra[t] - coef[t] * row_a
            rb[t] = rb[t] - coef[t] * row_b
        for m in range(j + 1, BLOCK):
            entry = rows_of(cols[m][v], s) * inverse
            for t in range(tiles):
                cols[m][t] = cols[m][t] - coef[t] * entry
    for u in range(min(tiles, len(a) - first - tiles)):
        for values, rows in ((a, ra), (b, rb)):
            terms = [
                below[j][u] * rows_of(rows[j // 8], j % 8) for j in range(BLOCK)
            ]
            while len(terms) > 1:
                terms = [x + y for x, y in zip(terms[::2], terms[1::2])]
            values[first + tiles + u] = values[first + tiles + u] - terms[0]
    if later < len(a):
        solved = jnp.concatenate([jnp.concatenate(ra, 0), jnp.concatenate(rb, 0)], 1)
        w_high, w_middle, w_low = split3(solved)
        right = jnp.concatenate([w_high, w_middle, w_low, w_high, w_middle, w_high], 0)
        change = jnp.dot(left, right.astype(BF16), preferred_element_type=F32)
        for t in range(later, len(a)):
            rows = slice(8 * (t - later), 8 * (t - later) + 8)
            a[t] = a[t] - change[rows, :128]
            b[t] = b[t] - change[rows, 128:]
    return jnp.concatenate(out, 0)


NT = (((1,), (1,)), ((), ()))


class Gathered:
    def __init__(self, masks, count, members, side_ref, own_ref):
        self.masks, self.count = masks, count
        self.me = lax.axis_index("blk") * members + lax.axis_index("grp")
        self.kind = parity(self.me, count)
        self.rows = own_ref.shape[1]
        self.dims = side_ref.shape[0] - 2
        self.vectors = own_ref.shape[0] - self.dims
        self.scale = side_ref[: self.dims, :]
        self.noise = side_ref[self.dims : self.dims + 1, :]
        self.pivots = side_ref[self.dims + 1 : self.dims + 2, :].astype(jnp.int32)
        self.points = lax.broadcasted_iota(jnp.int32, (self.rows, self.pivots.shape[1]), 0)
        self.own = own_ref[: self.dims, :] * self.scale
        self.left_own = left_stack(self.own).T.astype(BF16)

    def start(self):
        wide = jnp.zeros((self.rows, 2 * self.vectors), F32)
        narrow = jnp.zeros((self.rows, self.vectors), F32)
        return wide, narrow, jnp.zeros((3 * self.dims, self.pivots.shape[1]), F32)

    def owner(self, index, other):
        device, kind = self.me ^ other, self.kind ^ other
        for bit, (even, odd) in enumerate(zip(self.masks[0][:-1], self.masks[1][:-1])):
            device = device ^ (((index >> bit) & 1) * jnp.where(kind == 0, even, odd))
        return device

    def pick(self, total, ref, index, place, other):
        hots, parts = [], []
        for i in range(PICK):
            device = self.owner(place + index + i, other)
            hots.append((self.points == self.pivots - device * self.rows).astype(F32).astype(BF16))
            parts.append(jnp.concatenate(split3(ref[index + i, : self.dims, :]), 0).astype(BF16))
        return total + jnp.dot(
            jnp.concatenate(parts, 1), jnp.concatenate(hots, 0), preferred_element_type=F32
        )

    def add(self, wide, narrow, ref, index):
        blocks = [ref[index + i] for i in range(CHUNK)]
        right = jnp.concatenate(
            [right_stack(block[: self.dims] * self.scale) for block in blocks], 1
        )
        probe = jnp.concatenate([block[self.dims :] for block in blocks], 1)
        probe_high = probe.astype(BF16)
        probe_low = (probe - probe_high.astype(F32)).astype(BF16)
        value = matern(jnp.dot(self.left_own, right, preferred_element_type=F32))
        value_high = value.astype(BF16)
        value_low = (value - value_high.astype(F32)).astype(BF16)
        both = jnp.concatenate([probe_high, probe_low], 0)
        wide = wide + lax.dot_general(value_high, both, NT, preferred_element_type=F32)
        narrow = narrow + lax.dot_general(value_low, probe_high, NT, preferred_element_type=F32)
        return wide, narrow


def over(ref, width, carry, visit):
    steps = ref.shape[0] // width
    if ref.shape[0] <= UNROLL:
        for i in range(steps):
            carry = visit(carry, i * width)
        return carry
    return lax.fori_loop(0, steps, lambda i, c: visit(c, i * width), carry)


def partial_body(layout, place, side_ref, own_ref, part_ref, *refs):
    work = Gathered(*layout, side_ref, own_ref)
    wide, narrow, picked = work.start()
    if len(refs) > 3:
        wide, narrow, picked = [ref[...] for ref in refs[:3]]
    picked = over(part_ref, PICK, picked, lambda c, i: work.pick(c, part_ref, i, place, 0))
    wide, narrow = over(
        part_ref, CHUNK, (wide, narrow), lambda c, i: work.add(*c, part_ref, i)
    )
    refs[-3][...], refs[-2][...], refs[-1][...] = wide, narrow, picked


def last_body(
    layout, side_ref, own_ref, there_ref, wide_ref, narrow_ref, picked_ref,
    panel_ref, product_ref, rows_ref, total_ref, sems, total_sem,
):
    work = Gathered(*layout, side_ref, own_ref)
    picked = over(
        there_ref, PICK, picked_ref[...], lambda c, i: work.pick(c, there_ref, i, 0, 1)
    )
    dims = work.dims
    pivot_x = (picked[:dims] + picked[dims : 2 * dims] + picked[2 * dims :]) * work.scale
    size = pivot_x.shape[1]
    left_pivot = left_stack(pivot_x).T.astype(BF16)
    both = jnp.concatenate([right_stack(pivot_x), right_stack(work.own)], 1)
    values = matern(jnp.dot(left_pivot, both, preferred_element_type=F32))
    eye = lax.broadcasted_iota(jnp.int32, (size, size), 0) == lax.broadcasted_iota(
        jnp.int32, (size, size), 1
    )
    inner = values[:, :size] + jnp.where(eye, work.noise, 0.0)
    a = [inner[i : i + 8] for i in range(0, size, 8)]
    b = [values[i : i + 8, size:] for i in range(0, size, 8)]

    wide, narrow = wide_ref[...], narrow_ref[...]
    unrolled = there_ref.shape[0] <= UNROLL
    chunks = range(0, there_ref.shape[0], CHUNK) if unrolled else range(0)
    steps = size // BLOCK
    copies = []
    for step in range(steps):
        rows = pl.ds(step * BLOCK, BLOCK)
        rows_ref[rows, :] = eliminate(a, b, step)
        copies.append(
            pltpu.make_async_copy(rows_ref.at[rows, :], panel_ref.at[rows, :], sems.at[step])
        )
        copies[-1].start()
        for index in chunks[step::steps]:
            wide, narrow = work.add(wide, narrow, there_ref, index)
    if not unrolled:
        wide, narrow = over(
            there_ref, CHUNK, (wide, narrow), lambda c, i: work.add(*c, there_ref, i)
        )
    vectors = work.vectors
    total = wide[:, :vectors] + wide[:, vectors:] + narrow
    total_ref[...] = total.T + work.noise * own_ref[dims:, :]
    copies.append(pltpu.make_async_copy(total_ref, product_ref, total_sem))
    copies[-1].start()
    for copy in copies:
        copy.wait()


VMEM = pl.BlockSpec(memory_space=pltpu.VMEM)
PARAMS = pltpu.CompilerParams(vmem_limit_bytes=32 * 1024 * 1024)


def cost(points, rows):
    return pl.CostEstimate(
        flops=points * rows * 60, bytes_accessed=points * 100, transcendentals=points * rows * 2
    )


def partial(layout, place, side, own, part, *carry):
    rows, vectors = own.shape[1], own.shape[0] - side.shape[0] + 2
    return pl.pallas_call(
        functools.partial(partial_body, layout, place),
        out_shape=(
            jax.ShapeDtypeStruct((rows, 2 * vectors), F32),
            jax.ShapeDtypeStruct((rows, vectors), F32),
            jax.ShapeDtypeStruct((3 * (side.shape[0] - 2), side.shape[1]), F32),
        ),
        in_specs=[VMEM] * (3 + len(carry)),
        out_specs=(VMEM,) * 3,
        cost_estimate=cost(part.shape[0] * rows, rows),
        compiler_params=PARAMS,
    )(side, own, part, *carry)


def finish(layout, side, own, there, *carry):
    size, rows = side.shape[1], own.shape[1]
    product = (own.shape[0] - side.shape[0] + 2, rows)
    return pl.pallas_call(
        functools.partial(last_body, layout),
        out_shape=(
            jax.ShapeDtypeStruct((size, rows), F32),
            jax.ShapeDtypeStruct(product, F32),
        ),
        in_specs=[VMEM] * (3 + len(carry)),
        out_specs=(pl.BlockSpec(memory_space=pl.ANY),) * 2,
        scratch_shapes=[
            pltpu.VMEM((size, rows), F32),
            pltpu.VMEM(product, F32),
            pltpu.SemaphoreType.DMA((size // BLOCK,)),
            pltpu.SemaphoreType.DMA,
        ],
        compiler_params=PARAMS,
    )(side, own, there, *carry)


def solution(mesh):
    groups, members = mesh.shape["blk"], mesh.shape["grp"]
    count = groups * members
    masks = exchange_masks(groups, members)

    def swap(value, step):
        pairs = [(i, i ^ masks[parity(i, count)][step]) for i in range(count)]
        return lax.ppermute(value, ("blk", "grp"), pairs)

    def local(inputs, probes, lengths, noise, pivots):
        rows = inputs.shape[1]
        own = jnp.concatenate([inputs, probes], 0)
        layout = (masks, count, members)
        last = len(masks[0]) - 1
        here = own[None]
        for step in range(last - 1):
            if step == 1:
                side = jnp.concatenate(
                    [
                        jnp.broadcast_to((SCALE / lengths)[:, None], inputs.shape),
                        jnp.broadcast_to(noise[:, None], (1, rows)),
                        pivots.astype(F32)[None, :],
                    ],
                    0,
                )
            here = jnp.concatenate([here, swap(here, step)], 0)
        arrived = swap(here, last - 1)
        carry = partial(layout, 0, side, own, here)
        arrived, *carry = lax.optimization_barrier((arrived, *carry))
        there = swap(jnp.concatenate([here, arrived], 0), last)
        carry = partial(layout, here.shape[0], side, own, arrived, *carry)
        return finish(layout, side, own, there, *carry)

    in_specs = (P(None, ("blk", "grp")), P(None, ("blk", "grp")), P(), P(), P())
    out_specs = (P(None, ("blk", "grp")), P(None, ("blk", "grp")))
    return jax.shard_map(local, mesh=mesh, in_specs=in_specs, out_specs=out_specs, check_vma=False)
```

```python
import functools
import math

import jax
import jax.numpy as jnp
from jax import lax
from jax.experimental import pallas as pl
from jax.experimental.pallas import tpu as pltpu
from jax.sharding import PartitionSpec as P

F32 = jnp.float32
BF16 = jnp.bfloat16
LN2 = math.log(2.0)
SCALE = math.sqrt(5.0) / LN2
BLOCK = 16
CHUNK = 4
PICK = 2
UNROLL = 32


def exchange_masks(groups, members):
    low = members.bit_length() - 1
    bits = [1 << bit for bit in range(low - 1, 1, -1)]
    bits += [1 << (low + bit) for bit in range(groups.bit_length() - 2, -1, -1)]
    bits += [2] if members > 2 else []
    even = [bit | 1 for bit in bits]
    odd = even[:-2] + even[:-3:-1]
    return even + [1], odd + [1]


def parity(index, count):
    bits = 0
    for bit in range(count.bit_length() - 1):
        bits = bits ^ (index >> bit)
    return bits & 1


def split3(value):
    high = value.astype(BF16).astype(F32)
    rest = value - high
    middle = rest.astype(BF16).astype(F32)
    return high, middle, rest - middle


def norm_tile(x, first):
    high, middle, low = split3(jnp.sum(x * x, axis=0, keepdims=True))
    row = lax.broadcasted_iota(jnp.int32, x.shape, 0)
    if not first:
        row = jnp.where(row < 3, row + 3, row - 3)
    tile = jnp.where(row < 6, 1.0, 0.0)
    tile = jnp.where(row == 0, high, tile)
    tile = jnp.where(row == 1, middle, tile)
    return jnp.where(row == 2, low, tile)


def left_stack(x):
    high, middle, low = split3(x)
    return jnp.concatenate(
        [high, high, high, middle, middle, low, norm_tile(x, True), jnp.zeros_like(x)], 0
    )


def right_stack(x):
    high, middle, low = split3(-2.0 * x)
    return jnp.concatenate(
        [high, middle, low, high, middle, high, norm_tile(x, False), jnp.zeros_like(x)], 0
    ).astype(BF16)


def matern(square):
    square = jnp.maximum(square, 1e-30)
    radius = square * lax.rsqrt(square)
    return (1.0 + LN2 * radius + (LN2 * LN2 / 3.0) * square) * jnp.exp2(-radius)


def rows_of(value, row):
    return jnp.broadcast_to(value[row : row + 1, :], value.shape)


def eliminate(a, b, step):
    tiles = BLOCK // 8
    base, first = step * BLOCK, step * tiles
    later = first + 2 * tiles
    sub = lax.broadcasted_iota(jnp.int32, (8, 128), 0)

    def column(piece, m):
        return jnp.broadcast_to(piece[:, base + m : base + m + 1], (8, 128))

    ra, rb = a[first : first + tiles], b[first : first + tiles]
    cols = [[column(piece, m) for piece in ra] for m in range(BLOCK)]
    below = [[column(piece, m) for piece in a[first + tiles : later]] for m in range(BLOCK)]
    if later < len(a):
        l_high, l_middle, l_low = [
            part.astype(BF16) for part in split3(jnp.concatenate(a[later:], 0))
        ]
        left = jnp.concatenate([l_high, l_middle], 1)
    out = [jnp.zeros((8, 128), F32) for t in range(tiles)]
    for j in range(BLOCK):
        v, s = divmod(j, 8)
        pivot = rows_of(cols[j][v], s)
        inverse = 1.0 / pivot
        out[v] = jnp.where(sub == s, rb[v] * lax.rsqrt(pivot), out[v])
        coef = list(cols[j])
        coef[v] = coef[v] - jnp.where(sub == s, 1.0, 0.0)
        coef = [piece * inverse for piece in coef]
        row_a, row_b = rows_of(ra[v], s), rows_of(rb[v], s)
        for t in range(tiles):
            ra[t] = ra[t] - coef[t] * row_a
            rb[t] = rb[t] - coef[t] * row_b
        for m in range(j + 1, BLOCK):
            entry = rows_of(cols[m][v], s)
            for t in range(tiles):
                cols[m][t] = cols[m][t] - coef[t] * entry
    if first + tiles < len(a):
        for values, rows in ((a, ra), (b, rb)):
            sums = [[None, None] for u in range(tiles)]
            for j in range(BLOCK):
                row = rows_of(rows[j // 8], j % 8)
                for u in range(tiles):
                    term = below[j][u] * row
                    before = sums[u][j % 2]
                    sums[u][j % 2] = term if before is None else before + term
            for u in range(tiles):
                at = first + tiles + u
                values[at] = values[at] - (sums[u][0] + sums[u][1])
    if later < len(a):
        solved = jnp.concatenate([jnp.concatenate(ra, 0), jnp.concatenate(rb, 0)], 1)

        def placed(value):
            parts = [value.astype(BF16)]
            if base:
                parts.insert(0, jnp.zeros((base, value.shape[1]), BF16))
            parts.append(jnp.zeros((8 * len(a) - base - BLOCK, value.shape[1]), BF16))
            return jnp.concatenate(parts, 0)

        w_high, w_middle, w_low = [placed(part) for part in split3(solved)]
        change = (
            jnp.dot(left, jnp.concatenate([w_high, w_high], 0), preferred_element_type=F32)
            + jnp.dot(left, jnp.concatenate([w_middle, w_middle], 0), preferred_element_type=F32)
            + jnp.dot(
                jnp.concatenate([l_high, l_low], 1),
                jnp.concatenate([w_low, w_high], 0),
                preferred_element_type=F32,
            )
        )
        for t in range(later, len(a)):
            rows = slice(8 * (t - later), 8 * (t - later) + 8)
            a[t] = a[t] - change[rows, :128]
            b[t] = b[t] - change[rows, 128:]
    return jnp.concatenate(out, 0)


NT = (((1,), (1,)), ((), ()))


class Gathered:
    def __init__(self, masks, count, members, side_ref, own_ref, *mate_refs):
        self.masks, self.count = masks, count
        self.me = lax.axis_index("blk") * members + lax.axis_index("grp")
        self.kind = parity(self.me, count)
        self.rows = own_ref.shape[1]
        self.dims = side_ref.shape[0] - 2
        self.vectors = own_ref.shape[0] - self.dims
        self.scale = side_ref[: self.dims, :]
        self.noise = side_ref[self.dims : self.dims + 1, :]
        self.pivots = side_ref[self.dims + 1 : self.dims + 2, :].astype(jnp.int32)
        self.points = lax.broadcasted_iota(jnp.int32, (self.rows, self.pivots.shape[1]), 0)
        self.own = own_ref[: self.dims, :] * self.scale
        lefts = [left_stack(self.own)]
        lefts += [left_stack(ref[: self.dims, :] * self.scale) for ref in mate_refs]
        self.left_own = jnp.concatenate([left.T.astype(BF16) for left in lefts], 0)

    def start(self):
        wide = jnp.zeros((self.left_own.shape[0], 2 * self.vectors), F32)
        narrow = jnp.zeros((self.left_own.shape[0], self.vectors), F32)
        return wide, narrow, jnp.zeros((3 * self.dims, self.pivots.shape[1]), F32)

    def owner(self, index, other):
        device, kind = self.me ^ other, self.kind ^ other
        for bit, (even, odd) in enumerate(zip(self.masks[0][:-1], self.masks[1][:-1])):
            device = device ^ (((index >> bit) & 1) * jnp.where(kind == 0, even, odd))
        return device

    def pick(self, total, ref, index, place, other):
        hots, parts = [], []
        for i in range(PICK):
            device = self.owner(place + index + i, other)
            hots.append((self.points == self.pivots - device * self.rows).astype(F32).astype(BF16))
            parts.append(jnp.concatenate(split3(ref[index + i, : self.dims, :]), 0).astype(BF16))
        return total + jnp.dot(
            jnp.concatenate(parts, 1), jnp.concatenate(hots, 0), preferred_element_type=F32
        )

    def add(self, wide, narrow, ref, index):
        blocks = [ref[index + i] for i in range(CHUNK)]
        right = jnp.concatenate(
            [right_stack(block[: self.dims] * self.scale) for block in blocks], 1
        )
        probe = jnp.concatenate([block[self.dims :] for block in blocks], 1)
        probe_high = probe.astype(BF16)
        probe_low = (probe - probe_high.astype(F32)).astype(BF16)
        value = matern(jnp.dot(self.left_own, right, preferred_element_type=F32))
        value_high = value.astype(BF16)
        value_low = (value - value_high.astype(F32)).astype(BF16)
        both = jnp.concatenate([probe_high, probe_low], 0)
        wide = wide + lax.dot_general(value_high, both, NT, preferred_element_type=F32)
        narrow = narrow + lax.dot_general(value_low, probe_high, NT, preferred_element_type=F32)
        return wide, narrow


def over(blocks, width, carry, visit):
    steps = blocks // width
    if blocks <= UNROLL:
        for i in range(steps):
            carry = visit(carry, i * width)
        return carry
    return lax.fori_loop(0, steps, lambda i, c: visit(c, i * width), carry)


def gathered_sum(wide, narrow):
    vectors = narrow.shape[1]
    return (wide[:, :vectors] + wide[:, vectors:] + narrow).T


def early_body(layout, side_ref, own_ref, mate_ref, part_ref, wide_ref, narrow_ref, picked_ref, parcel_ref):
    work = Gathered(*layout, side_ref, own_ref, mate_ref)
    wide, narrow, picked = work.start()
    blocks, rows = part_ref.shape[0], work.rows
    picked = over(blocks, PICK, picked, lambda c, i: work.pick(c, part_ref, i, 0, 0))
    wide, narrow = over(blocks, CHUNK, (wide, narrow), lambda c, i: work.add(*c, part_ref, i))
    wide_ref[...], narrow_ref[...], picked_ref[...] = wide[:rows], narrow[:rows], picked
    parcel_ref[0, : work.vectors, :] = gathered_sum(wide[rows:], narrow[rows:])
    parcel_ref[0, work.vectors :, :] = jnp.zeros((work.dims, rows), F32)
    parcel_ref[1] = picked


def middle_body(
    layout, place, side_ref, own_ref, part_ref, wide_in, narrow_in, picked_in,
    wide_ref, narrow_ref, picked_ref,
):
    work = Gathered(*layout, side_ref, own_ref)
    blocks = part_ref.shape[0]
    picked_ref[...] = over(
        blocks, PICK, picked_in[...], lambda c, i: work.pick(c, part_ref, i, place, 0)
    )
    wide_ref[...], narrow_ref[...] = over(
        blocks, CHUNK, (wide_in[...], narrow_in[...]), lambda c, i: work.add(*c, part_ref, i)
    )


def last_body(
    layout, side_ref, own_ref, there_ref, wide_ref, narrow_ref, picked_ref,
    panel_ref, product_ref, rows_ref, total_ref, sems, total_sem,
):
    work = Gathered(*layout, side_ref, own_ref)
    blocks = there_ref.shape[0] - 2
    picked = over(
        blocks,
        PICK,
        picked_ref[...] + there_ref[blocks + 1],
        lambda c, i: work.pick(c, there_ref, i, blocks, 1),
    )
    dims = work.dims
    pivot_x = (picked[:dims] + picked[dims : 2 * dims] + picked[2 * dims :]) * work.scale
    size = pivot_x.shape[1]
    left_pivot = left_stack(pivot_x).T.astype(BF16)
    both = jnp.concatenate([right_stack(pivot_x), right_stack(work.own)], 1)
    values = matern(jnp.dot(left_pivot, both, preferred_element_type=F32))
    eye = lax.broadcasted_iota(jnp.int32, (size, size), 0) == lax.broadcasted_iota(
        jnp.int32, (size, size), 1
    )
    inner = values[:, :size] + jnp.where(eye, work.noise, 0.0)
    a = [inner[i : i + 8] for i in range(0, size, 8)]
    b = [values[i : i + 8, size:] for i in range(0, size, 8)]

    wide, narrow = wide_ref[...], narrow_ref[...]
    chunks = range(0, blocks, CHUNK) if blocks <= UNROLL else range(0)
    if blocks > UNROLL:
        wide, narrow = over(
            blocks, CHUNK, (wide, narrow), lambda c, i: work.add(*c, there_ref, i)
        )
    steps = size // BLOCK
    copies = []
    for step in range(steps):
        rows = pl.ds(step * BLOCK, BLOCK)
        rows_ref[rows, :] = eliminate(a, b, step)
        copies.append(
            pltpu.make_async_copy(rows_ref.at[rows, :], panel_ref.at[rows, :], sems.at[step])
        )
        copies[-1].start()
        for index in chunks[step::steps]:
            wide, narrow = work.add(wide, narrow, there_ref, index)
        if step == min(len(chunks), steps - 1):
            total = gathered_sum(wide, narrow) + there_ref[blocks, : work.vectors, :]
            total_ref[...] = total + work.noise * own_ref[dims:, :]
            copies.append(pltpu.make_async_copy(total_ref, product_ref, total_sem))
            copies[-1].start()
    for copy in copies:
        copy.wait()


VMEM = pl.BlockSpec(memory_space=pltpu.VMEM)
PARAMS = pltpu.CompilerParams(vmem_limit_bytes=32 * 1024 * 1024)


def cost(points, rows):
    return pl.CostEstimate(
        flops=points * rows * 60, bytes_accessed=points * 100, transcendentals=points * rows * 2
    )


def sums(side, own):
    rows, vectors = own.shape[1], own.shape[0] - side.shape[0] + 2
    return (
        jax.ShapeDtypeStruct((rows, 2 * vectors), F32),
        jax.ShapeDtypeStruct((rows, vectors), F32),
        jax.ShapeDtypeStruct((3 * (side.shape[0] - 2), side.shape[1]), F32),
    )


def early(layout, side, own, mate, part):
    rows = own.shape[1]
    return pl.pallas_call(
        functools.partial(early_body, layout),
        out_shape=sums(side, own) + (jax.ShapeDtypeStruct((2,) + own.shape, F32),),
        in_specs=[VMEM] * 4,
        out_specs=(VMEM,) * 4,
        cost_estimate=cost(part.shape[0] * rows, 2 * rows),
        compiler_params=PARAMS,
    )(side, own, mate, part)


def middle(layout, place, side, own, part, *carry):
    rows = own.shape[1]
    return pl.pallas_call(
        functools.partial(middle_body, layout, place),
        out_shape=sums(side, own),
        in_specs=[VMEM] * 6,
        out_specs=(VMEM,) * 3,
        cost_estimate=cost(part.shape[0] * rows, rows),
        compiler_params=PARAMS,
    )(side, own, part, *carry)


def finish(layout, side, own, there, *carry):
    size, rows = side.shape[1], own.shape[1]
    product = (own.shape[0] - side.shape[0] + 2, rows)
    return pl.pallas_call(
        functools.partial(last_body, layout),
        out_shape=(
            jax.ShapeDtypeStruct((size, rows), F32),
            jax.ShapeDtypeStruct(product, F32),
        ),
        in_specs=[VMEM] * (3 + len(carry)),
        out_specs=(pl.BlockSpec(memory_space=pl.ANY),) * 2,
        scratch_shapes=[
            pltpu.VMEM((size, rows), F32),
            pltpu.VMEM(product, F32),
            pltpu.SemaphoreType.DMA((size // BLOCK,)),
            pltpu.SemaphoreType.DMA,
        ],
        compiler_params=PARAMS,
    )(side, own, there, *carry)


def solution(mesh):
    groups, members = mesh.shape["blk"], mesh.shape["grp"]
    count = groups * members
    masks = exchange_masks(groups, members)

    def swap(value, step):
        pairs = [(i, i ^ masks[parity(i, count)][step]) for i in range(count)]
        return lax.ppermute(value, ("blk", "grp"), pairs)

    def local(inputs, probes, lengths, noise, pivots):
        rows = inputs.shape[1]
        own = jnp.concatenate([inputs, probes], 0)
        layout = (masks, count, members)
        last = len(masks[0]) - 1
        here = own[None]
        for step in range(last - 1):
            if step == 1:
                side = jnp.concatenate(
                    [
                        jnp.broadcast_to((SCALE / lengths)[:, None], inputs.shape),
                        jnp.broadcast_to(noise[:, None], (1, rows)),
                        pivots.astype(F32)[None, :],
                    ],
                    0,
                )
            if step == 1:
                mate = swap(lax.optimization_barrier((own, here))[0], last)
            here = jnp.concatenate([here, swap(here, step)], 0)
        arrived = swap(here, last - 1)
        *carry, parcel = early(layout, side, own, mate, here)
        arrived, parcel = lax.optimization_barrier((arrived, parcel))
        there = swap(jnp.concatenate([arrived, parcel], 0), last)
        carry = middle(layout, here.shape[0], side, own, arrived, *carry)
        return finish(layout, side, own, there, *carry)

    in_specs = (P(None, ("blk", "grp")), P(None, ("blk", "grp")), P(), P(), P())
    out_specs = (P(None, ("blk", "grp")), P(None, ("blk", "grp")))
    return jax.shard_map(local, mesh=mesh, in_specs=in_specs, out_specs=out_specs, check_vma=False)
```

```python
import functools
import math

import jax
import jax.numpy as jnp
from jax import lax
from jax.experimental import pallas as pl
from jax.experimental.pallas import tpu as pltpu
from jax.sharding import PartitionSpec as P

F32 = jnp.float32
BF16 = jnp.bfloat16
LN2 = math.log(2.0)
SCALE = math.sqrt(5.0) / LN2
BLOCK = 16
CHUNK = 4
PICK = 2
FIRST = 5
UNROLL = 32


def exchange_masks(groups, members):
    low = members.bit_length() - 1
    bits = [1 << bit for bit in range(low - 1, 1, -1)]
    bits += [1 << (low + bit) for bit in range(groups.bit_length() - 2, -1, -1)]
    bits += [2] if members > 2 else []
    even = [bit | 1 for bit in bits]
    odd = even[:-2] + even[:-3:-1]
    return even + [1], odd + [1]


def parity(index, count):
    bits = 0
    for bit in range(count.bit_length() - 1):
        bits = bits ^ (index >> bit)
    return bits & 1


def split3(value):
    high = value.astype(BF16).astype(F32)
    rest = value - high
    middle = rest.astype(BF16).astype(F32)
    return high, middle, rest - middle


def norm_tile(x, first):
    high, middle, low = split3(jnp.sum(x * x, axis=0, keepdims=True))
    row = lax.broadcasted_iota(jnp.int32, x.shape, 0)
    if not first:
        row = jnp.where(row < 3, row + 3, row - 3)
    tile = jnp.where(row < 6, 1.0, 0.0)
    tile = jnp.where(row == 0, high, tile)
    tile = jnp.where(row == 1, middle, tile)
    return jnp.where(row == 2, low, tile)


def left_stack(x):
    high, middle, low = split3(x)
    return jnp.concatenate(
        [high, high, high, middle, middle, low, norm_tile(x, True), jnp.zeros_like(x)], 0
    )


def right_stack(x):
    high, middle, low = split3(-2.0 * x)
    return jnp.concatenate(
        [high, middle, low, high, middle, high, norm_tile(x, False), jnp.zeros_like(x)], 0
    ).astype(BF16)


def matern(square):
    square = jnp.maximum(square, 1e-30)
    radius = square * lax.rsqrt(square)
    return (1.0 + LN2 * radius + (LN2 * LN2 / 3.0) * square) * jnp.exp2(-radius)


def rows_of(value, row):
    return jnp.broadcast_to(value[row : row + 1, :], value.shape)


def eliminate(a, b, step):
    tiles = BLOCK // 8
    base, first = step * BLOCK, step * tiles
    later = first + 2 * tiles
    sub = lax.broadcasted_iota(jnp.int32, (8, 128), 0)

    def column(piece, m):
        return jnp.broadcast_to(piece[:, base + m : base + m + 1], (8, 128))

    ra, rb = a[first : first + tiles], b[first : first + tiles]
    cols = [[column(piece, m) for piece in ra] for m in range(BLOCK)]
    below = [[column(piece, m) for piece in a[first + tiles : later]] for m in range(BLOCK)]
    if later < len(a):
        l_high, l_middle, l_low = [
            part.astype(BF16) for part in split3(jnp.concatenate(a[later:], 0))
        ]
        left = jnp.concatenate([l_high, l_middle], 1)
    out = [jnp.zeros((8, 128), F32) for t in range(tiles)]
    for j in range(0, BLOCK, 2):
        v, s = divmod(j, 8)
        one, two = cols[j], cols[j + 1]
        top, side, end = rows_of(one[v], s), rows_of(one[v], s + 1), rows_of(two[v], s + 1)
        det = top * end - side * side
        inverse = 1.0 / det
        row_a, next_a = rows_of(ra[v], s), rows_of(ra[v], s + 1)
        row_b, next_b = rows_of(rb[v], s), rows_of(rb[v], s + 1)
        root = lax.rsqrt(top)
        out[v] = jnp.where(sub == s, row_b * root, out[v])
        out[v] = jnp.where(
            sub == s + 1, (top * next_b - side * row_b) * (root * lax.rsqrt(det)), out[v]
        )
        one, two = list(one), list(two)
        one[v] = one[v] - jnp.where(sub == s, 1.0, 0.0)
        two[v] = two[v] - jnp.where(sub == s + 1, 1.0, 0.0)
        first_coef = [(x * end - y * side) * inverse for x, y in zip(one, two)]
        next_coef = [(y * top - x * side) * inverse for x, y in zip(one, two)]
        for t in range(tiles):
            ra[t] = ra[t] - first_coef[t] * row_a - next_coef[t] * next_a
            rb[t] = rb[t] - first_coef[t] * row_b - next_coef[t] * next_b
        for m in range(j + 2, BLOCK):
            entry, following = rows_of(cols[m][v], s), rows_of(cols[m][v], s + 1)
            for t in range(tiles):
                change = first_coef[t] * entry + next_coef[t] * following
                cols[m][t] = cols[m][t] - change
    if first + tiles < len(a):
        for values, rows in ((a, ra), (b, rb)):
            sums = [[None, None] for u in range(tiles)]
            for j in range(BLOCK):
                row = rows_of(rows[j // 8], j % 8)
                for u in range(tiles):
                    term = below[j][u] * row
                    before = sums[u][j % 2]
                    sums[u][j % 2] = term if before is None else before + term
            for u in range(tiles):
                at = first + tiles + u
                values[at] = values[at] - (sums[u][0] + sums[u][1])
    if later < len(a):
        solved = jnp.concatenate([jnp.concatenate(ra, 0), jnp.concatenate(rb, 0)], 1)

        def placed(value):
            parts = [value.astype(BF16)]
            if base:
                parts.insert(0, jnp.zeros((base, value.shape[1]), BF16))
            parts.append(jnp.zeros((8 * len(a) - base - BLOCK, value.shape[1]), BF16))
            return jnp.concatenate(parts, 0)

        w_high, w_middle, w_low = [placed(part) for part in split3(solved)]
        change = (
            jnp.dot(left, jnp.concatenate([w_high, w_high], 0), preferred_element_type=F32)
            + jnp.dot(left, jnp.concatenate([w_middle, w_middle], 0), preferred_element_type=F32)
            + jnp.dot(
                jnp.concatenate([l_high, l_low], 1),
                jnp.concatenate([w_low, w_high], 0),
                preferred_element_type=F32,
            )
        )
        for t in range(later, len(a)):
            rows = slice(8 * (t - later), 8 * (t - later) + 8)
            a[t] = a[t] - change[rows, :128]
            b[t] = b[t] - change[rows, 128:]
    return jnp.concatenate(out, 0)


NT = (((1,), (1,)), ((), ()))


class Gathered:
    def __init__(self, layout, side_ref, own_ref):
        self.masks, self.count, members = layout
        self.me = lax.axis_index("blk") * members + lax.axis_index("grp")
        self.kind = parity(self.me, self.count)
        self.dims, self.rows = own_ref.shape
        self.scale = side_ref[: self.dims, :]
        self.noise = side_ref[self.dims : self.dims + 1, :]
        self.pivots = side_ref[self.dims + 1 : self.dims + 2, :].astype(jnp.int32)
        self.points = lax.broadcasted_iota(jnp.int32, (self.rows, self.pivots.shape[1]), 0)
        self.own = own_ref[...] * self.scale

    def owner(self, index, other):
        device, kind = self.me ^ other, self.kind ^ other
        for bit, (even, odd) in enumerate(zip(self.masks[0][:-1], self.masks[1][:-1])):
            device = device ^ (((index >> bit) & 1) * jnp.where(kind == 0, even, odd))
        return device

    def pick(self, total, ref, other):
        def visit(total, index):
            hots, parts = [], []
            for i in range(PICK):
                device = self.owner(index + i, other)
                hot = self.points == self.pivots - device * self.rows
                hots.append(hot.astype(F32).astype(BF16))
                parts.append(jnp.concatenate(split3(ref[index + i]), 0).astype(BF16))
            return total + jnp.dot(
                jnp.concatenate(parts, 1), jnp.concatenate(hots, 0), preferred_element_type=F32
            )

        return over(ref.shape[0], PICK, total, visit)

    def left(self):
        return left_stack(self.own).T.astype(BF16)

    def product(self, carry, points_ref, probes_ref):
        left_own = self.left()

        def visit(carry, index):
            wide, narrow = carry
            places = [index + i for i in range(CHUNK)]
            right = jnp.concatenate(
                [right_stack(points_ref[place] * self.scale) for place in places], 1
            )
            probe = jnp.concatenate([probes_ref[place] for place in places], 1)
            probe_high = probe.astype(BF16)
            probe_low = (probe - probe_high.astype(F32)).astype(BF16)
            value = matern(jnp.dot(left_own, right, preferred_element_type=F32))
            value_high = value.astype(BF16)
            value_low = (value - value_high.astype(F32)).astype(BF16)
            both = jnp.concatenate([probe_high, probe_low], 0)
            wide = wide + lax.dot_general(value_high, both, NT, preferred_element_type=F32)
            narrow = narrow + lax.dot_general(value_low, probe_high, NT, preferred_element_type=F32)
            return wide, narrow

        return over(points_ref.shape[0], CHUNK, carry, visit)


def over(blocks, width, carry, visit):
    steps = blocks // width
    if blocks <= UNROLL:
        for i in range(steps):
            carry = visit(carry, i * width)
        return carry
    return lax.fori_loop(0, steps, lambda i, c: visit(c, i * width), carry)


def pick_body(layout, side_ref, own_ref, points_ref, picked_ref):
    work = Gathered(layout, side_ref, own_ref)
    zero = jnp.zeros((3 * work.dims, side_ref.shape[1]), F32)
    picked_ref[...] = work.pick(zero, points_ref, 0)


def pivot_body(layout, side_ref, own_ref, points_ref, picked_ref, a_ref, b_ref):
    work = Gathered(layout, side_ref, own_ref)
    picked = work.pick(picked_ref[...], points_ref, 1)
    dims = work.dims
    pivot_x = (picked[:dims] + picked[dims : 2 * dims] + picked[2 * dims :]) * work.scale
    size = pivot_x.shape[1]
    left_pivot = left_stack(pivot_x).T.astype(BF16)
    both = jnp.concatenate([right_stack(pivot_x), right_stack(work.own)], 1)
    values = matern(jnp.dot(left_pivot, both, preferred_element_type=F32))
    eye = lax.broadcasted_iota(jnp.int32, (size, size), 0) == lax.broadcasted_iota(
        jnp.int32, (size, size), 1
    )
    a_ref[...] = values[:, :size] + jnp.where(eye, work.noise, 0.0)
    b_ref[...] = values[:, size:]


def first_body(
    layout, side_ref, own_ref, points_ref, probes_ref, a_ref, b_ref,
    a_out, b_out, rows_ref, wide_ref, narrow_ref,
):
    work = Gathered(layout, side_ref, own_ref)
    vectors = probes_ref.shape[1]
    carry = jnp.zeros((work.rows, 2 * vectors), F32), jnp.zeros((work.rows, vectors), F32)
    wide_ref[...], narrow_ref[...] = work.product(carry, points_ref, probes_ref)
    size, done = a_ref.shape[0], rows_ref.shape[0]
    a = [a_ref[i : i + 8, :] for i in range(0, size, 8)]
    b = [b_ref[i : i + 8, :] for i in range(0, size, 8)]
    for step in range(done // BLOCK):
        rows_ref[step * BLOCK : (step + 1) * BLOCK, :] = eliminate(a, b, step)
    a_out[...] = jnp.concatenate(a[done // 8 :], 0)
    b_out[...] = jnp.concatenate(b[done // 8 :], 0)


def last_body(
    layout, side_ref, own_ref, points_ref, probes_ref, own_probes_ref,
    a_ref, b_ref, done_ref, wide_ref, narrow_ref,
    panel_ref, product_ref, rows_ref, total_ref, sems,
):
    done = done_ref.shape[0]
    copies = [pltpu.make_async_copy(done_ref, panel_ref.at[pl.ds(0, done), :], sems.at[0])]
    copies[-1].start()
    work = Gathered(layout, side_ref, own_ref)
    wide, narrow = work.product((wide_ref[...], narrow_ref[...]), points_ref, probes_ref)
    vectors = narrow.shape[1]
    total = (wide[:, :vectors] + wide[:, vectors:] + narrow).T
    total_ref[...] = total + work.noise * own_probes_ref[...]
    copies.append(pltpu.make_async_copy(total_ref, product_ref, sems.at[1]))
    left = rows_ref.shape[0]
    a = [None] * (done // 8) + [a_ref[i : i + 8, :] for i in range(0, left, 8)]
    b = [None] * (done // 8) + [b_ref[i : i + 8, :] for i in range(0, left, 8)]
    for step in range(left // BLOCK):
        rows_ref[step * BLOCK : (step + 1) * BLOCK, :] = eliminate(a, b, done // BLOCK + step)
        if step == left // BLOCK - 2:
            copies[-1].start()
    copies.append(
        pltpu.make_async_copy(rows_ref, panel_ref.at[pl.ds(done, left), :], sems.at[2])
    )
    copies[-1].start()
    for copy in copies:
        copy.wait()


VMEM = pl.BlockSpec(memory_space=pltpu.VMEM)
ANY = pl.BlockSpec(memory_space=pl.ANY)
PARAMS = pltpu.CompilerParams(vmem_limit_bytes=32 * 1024 * 1024)


def shapes(*dims):
    return tuple(jax.ShapeDtypeStruct(dim, F32) for dim in dims)


def run(body, layout, outs, args, work, spec=VMEM, scratch=()):
    cost = pl.CostEstimate(flops=work * 60, bytes_accessed=work // 4, transcendentals=work * 2)
    return pl.pallas_call(
        functools.partial(body, layout),
        out_shape=shapes(*outs),
        in_specs=[VMEM] * len(args),
        out_specs=(spec,) * len(outs),
        scratch_shapes=scratch,
        cost_estimate=cost,
        compiler_params=PARAMS,
    )(*args)


def solution(mesh):
    groups, members = mesh.shape["blk"], mesh.shape["grp"]
    count = groups * members
    masks = exchange_masks(groups, members)
    layout = (masks, count, members)
    last = len(masks[0]) - 1

    def swap(value, step):
        pairs = [(i, i ^ masks[parity(i, count)][step]) for i in range(count)]
        return lax.ppermute(value, ("blk", "grp"), pairs)

    def local(inputs, probes, lengths, noise, pivots):
        rows, vectors, size = inputs.shape[1], probes.shape[0], pivots.shape[0]
        points, vector = inputs[None], probes[None]
        for step in range(last):
            if step == 1:
                side = jnp.concatenate(
                    [
                        jnp.broadcast_to((SCALE / lengths)[:, None], inputs.shape),
                        jnp.broadcast_to(noise[:, None], (1, rows)),
                        pivots.astype(F32)[None, :],
                    ],
                    0,
                )
            came = swap(points, step)
            vector_came = swap(vector, step)
            points = jnp.concatenate([points, came], 0)
            if step < last - 1:
                vector = jnp.concatenate([vector, vector_came], 0)
                vector = lax.optimization_barrier((vector, came))[0]
        points_there = swap(points, last)
        picked, = run(
            pick_body, layout, [(3 * inputs.shape[0], size)], (side, inputs, points), size * rows
        )
        a, b = run(
            pivot_body, layout, [(size, size), (size, rows)],
            (side, inputs, points_there, picked), size * rows,
        )
        vector_came, a = lax.optimization_barrier((vector_came, a))
        vector = jnp.concatenate([vector, vector_came], 0)
        vector_there = swap(vector, last)
        done = FIRST * BLOCK
        a, b, done_rows, wide, narrow = run(
            first_body, layout,
            [(size - done, size), (size - done, rows), (done, rows), (rows, 2 * vectors), (rows, vectors)],
            (side, inputs, points, vector, a, b), size * rows * 16,
        )
        return run(
            last_body, layout, [(size, rows), (vectors, rows)],
            (side, inputs, points_there, vector_there, probes, a, b, done_rows, wide, narrow),
            size * rows * 16, ANY,
            [
                pltpu.VMEM((size - done, rows), F32),
                pltpu.VMEM((vectors, rows), F32),
                pltpu.SemaphoreType.DMA((3,)),
            ],
        )

    in_specs = (P(None, ("blk", "grp")), P(None, ("blk", "grp")), P(), P(), P())
    out_specs = (P(None, ("blk", "grp")), P(None, ("blk", "grp")))
    return jax.shard_map(local, mesh=mesh, in_specs=in_specs, out_specs=out_specs, check_vma=False)
```

```python
import functools
import math

import jax
import jax.numpy as jnp
from jax import lax
from jax.experimental import pallas as pl
from jax.experimental.pallas import tpu as pltpu
from jax.sharding import PartitionSpec as P

F32 = jnp.float32
BF16 = jnp.bfloat16
LN2 = math.log(2.0)
SCALE = math.sqrt(5.0) / LN2
BLOCK = 16
CHUNK = 4
PICK = 2
UNROLL = 32


def exchange_masks(groups, members):
    low = members.bit_length() - 1
    bits = [1 << bit for bit in range(low - 1, 1, -1)]
    bits += [1 << (low + bit) for bit in range(groups.bit_length() - 2, -1, -1)]
    bits += [2] if members > 2 else []
    even = [bit | 1 for bit in bits]
    odd = even[:-2] + even[:-3:-1]
    return even + [1], odd + [1]


def parity(index, count):
    bits = 0
    for bit in range(count.bit_length() - 1):
        bits = bits ^ (index >> bit)
    return bits & 1


def split3(value):
    high = value.astype(BF16).astype(F32)
    rest = value - high
    middle = rest.astype(BF16).astype(F32)
    return high, middle, rest - middle


def norm_tile(x, first):
    high, middle, low = split3(jnp.sum(x * x, axis=0, keepdims=True))
    row = lax.broadcasted_iota(jnp.int32, x.shape, 0)
    if not first:
        row = jnp.where(row < 3, row + 3, row - 3)
    tile = jnp.where(row < 6, 1.0, 0.0)
    tile = jnp.where(row == 0, high, tile)
    tile = jnp.where(row == 1, middle, tile)
    return jnp.where(row == 2, low, tile)


def left_stack(x):
    high, middle, low = split3(x)
    return jnp.concatenate(
        [high, high, high, middle, middle, low, norm_tile(x, True), jnp.zeros_like(x)], 0
    )


def right_stack(x):
    high, middle, low = split3(-2.0 * x)
    return jnp.concatenate(
        [high, middle, low, high, middle, high, norm_tile(x, False), jnp.zeros_like(x)], 0
    ).astype(BF16)


def matern(square):
    square = jnp.maximum(square, 1e-30)
    radius = square * lax.rsqrt(square)
    return (1.0 + LN2 * radius + (LN2 * LN2 / 3.0) * square) * jnp.exp2(-radius)


def rows_of(value, row):
    return jnp.broadcast_to(value[row : row + 1, :], value.shape)


def eliminate(a, b, step):
    tiles = BLOCK // 8
    base, first = step * BLOCK, step * tiles
    later = first + 2 * tiles
    sub = lax.broadcasted_iota(jnp.int32, (8, 128), 0)

    def column(piece, m):
        return jnp.broadcast_to(piece[:, base + m : base + m + 1], (8, 128))

    ra, rb = a[first : first + tiles], b[first : first + tiles]
    cols = [[column(piece, m) for piece in ra] for m in range(BLOCK)]
    below = [[column(piece, m) for piece in a[first + tiles : later]] for m in range(BLOCK)]
    if later < len(a):
        l_high, l_middle, l_low = [
            part.astype(BF16) for part in split3(jnp.concatenate(a[later:], 0))
        ]
        left = jnp.concatenate([l_high, l_middle], 1)
    out = [jnp.zeros((8, 128), F32) for t in range(tiles)]
    for j in range(0, BLOCK, 2):
        v, s = divmod(j, 8)
        one, two = cols[j], cols[j + 1]
        top, side, end = rows_of(one[v], s), rows_of(one[v], s + 1), rows_of(two[v], s + 1)
        det = top * end - side * side
        inverse = 1.0 / det
        row_a, next_a = rows_of(ra[v], s), rows_of(ra[v], s + 1)
        row_b, next_b = rows_of(rb[v], s), rows_of(rb[v], s + 1)
        root = lax.rsqrt(top)
        out[v] = jnp.where(sub == s, row_b * root, out[v])
        out[v] = jnp.where(
            sub == s + 1, (top * next_b - side * row_b) * (root * lax.rsqrt(det)), out[v]
        )
        one, two = list(one), list(two)
        one[v] = one[v] - jnp.where(sub == s, 1.0, 0.0)
        two[v] = two[v] - jnp.where(sub == s + 1, 1.0, 0.0)
        first_coef = [(x * end - y * side) * inverse for x, y in zip(one, two)]
        next_coef = [(y * top - x * side) * inverse for x, y in zip(one, two)]
        for t in range(tiles):
            ra[t] = ra[t] - first_coef[t] * row_a - next_coef[t] * next_a
            rb[t] = rb[t] - first_coef[t] * row_b - next_coef[t] * next_b
        for m in range(j + 2, BLOCK):
            entry, following = rows_of(cols[m][v], s), rows_of(cols[m][v], s + 1)
            for t in range(tiles):
                change = first_coef[t] * entry + next_coef[t] * following
                cols[m][t] = cols[m][t] - change
    if first + tiles < len(a):
        for values, rows in ((a, ra), (b, rb)):
            sums = [[None, None] for u in range(tiles)]
            for j in range(BLOCK):
                row = rows_of(rows[j // 8], j % 8)
                for u in range(tiles):
                    term = below[j][u] * row
                    before = sums[u][j % 2]
                    sums[u][j % 2] = term if before is None else before + term
            for u in range(tiles):
                at = first + tiles + u
                values[at] = values[at] - (sums[u][0] + sums[u][1])
    if later < len(a):
        solved = jnp.concatenate([jnp.concatenate(ra, 0), jnp.concatenate(rb, 0)], 1)

        def placed(value):
            parts = [value.astype(BF16)]
            if base:
                parts.insert(0, jnp.zeros((base, value.shape[1]), BF16))
            parts.append(jnp.zeros((8 * len(a) - base - BLOCK, value.shape[1]), BF16))
            return jnp.concatenate(parts, 0)

        w_high, w_middle, w_low = [placed(part) for part in split3(solved)]
        change = (
            jnp.dot(left, jnp.concatenate([w_high, w_high], 0), preferred_element_type=F32)
            + jnp.dot(left, jnp.concatenate([w_middle, w_middle], 0), preferred_element_type=F32)
            + jnp.dot(
                jnp.concatenate([l_high, l_low], 1),
                jnp.concatenate([w_low, w_high], 0),
                preferred_element_type=F32,
            )
        )
        for t in range(later, len(a)):
            rows = slice(8 * (t - later), 8 * (t - later) + 8)
            a[t] = a[t] - change[rows, :128]
            b[t] = b[t] - change[rows, 128:]
    return jnp.concatenate(out, 0)


NT = (((1,), (1,)), ((), ()))


class Gathered:
    def __init__(self, masks, count, members, side_ref, own_ref, *mate_refs):
        self.masks, self.count = masks, count
        self.me = lax.axis_index("blk") * members + lax.axis_index("grp")
        self.kind = parity(self.me, count)
        self.rows = own_ref.shape[1]
        self.dims = side_ref.shape[0] - 2
        self.vectors = own_ref.shape[0] - self.dims
        self.scale = side_ref[: self.dims, :]
        self.noise = side_ref[self.dims : self.dims + 1, :]
        self.pivots = side_ref[self.dims + 1 : self.dims + 2, :].astype(jnp.int32)
        self.points = lax.broadcasted_iota(jnp.int32, (self.rows, self.pivots.shape[1]), 0)
        self.own = own_ref[: self.dims, :] * self.scale
        lefts = [left_stack(self.own)]
        lefts += [left_stack(ref[: self.dims, :] * self.scale) for ref in mate_refs]
        self.left_own = jnp.concatenate([left.T.astype(BF16) for left in lefts], 0)

    def start(self):
        wide = jnp.zeros((self.left_own.shape[0], 2 * self.vectors), F32)
        narrow = jnp.zeros((self.left_own.shape[0], self.vectors), F32)
        return wide, narrow, jnp.zeros((3 * self.dims, self.pivots.shape[1]), F32)

    def owner(self, index, other):
        device, kind = self.me ^ other, self.kind ^ other
        for bit, (even, odd) in enumerate(zip(self.masks[0][:-1], self.masks[1][:-1])):
            device = device ^ (((index >> bit) & 1) * jnp.where(kind == 0, even, odd))
        return device

    def pick(self, total, ref, index, place, other):
        hots, parts = [], []
        for i in range(PICK):
            device = self.owner(place + index + i, other)
            hots.append((self.points == self.pivots - device * self.rows).astype(F32).astype(BF16))
            parts.append(jnp.concatenate(split3(ref[index + i, : self.dims, :]), 0).astype(BF16))
        return total + jnp.dot(
            jnp.concatenate(parts, 1), jnp.concatenate(hots, 0), preferred_element_type=F32
        )

    def add(self, wide, narrow, ref, index):
        blocks = [ref[index + i] for i in range(CHUNK)]
        right = jnp.concatenate(
            [right_stack(block[: self.dims] * self.scale) for block in blocks], 1
        )
        probe = jnp.concatenate([block[self.dims :] for block in blocks], 1)
        probe_high = probe.astype(BF16)
        probe_low = (probe - probe_high.astype(F32)).astype(BF16)
        value = matern(jnp.dot(self.left_own, right, preferred_element_type=F32))
        value_high = value.astype(BF16)
        value_low = (value - value_high.astype(F32)).astype(BF16)
        both = jnp.concatenate([probe_high, probe_low], 0)
        wide = wide + lax.dot_general(value_high, both, NT, preferred_element_type=F32)
        narrow = narrow + lax.dot_general(value_low, probe_high, NT, preferred_element_type=F32)
        return wide, narrow


def over(blocks, width, carry, visit):
    steps = blocks // width
    if blocks <= UNROLL:
        for i in range(steps):
            carry = visit(carry, i * width)
        return carry
    return lax.fori_loop(0, steps, lambda i, c: visit(c, i * width), carry)


def gathered_sum(wide, narrow):
    vectors = narrow.shape[1]
    return (wide[:, :vectors] + wide[:, vectors:] + narrow).T


def early_body(layout, side_ref, own_ref, mate_ref, part_ref, wide_ref, narrow_ref, picked_ref, parcel_ref):
    work = Gathered(*layout, side_ref, own_ref, mate_ref)
    wide, narrow, picked = work.start()
    blocks, rows = part_ref.shape[0], work.rows
    picked = over(blocks, PICK, picked, lambda c, i: work.pick(c, part_ref, i, 0, 0))
    wide, narrow = over(blocks, CHUNK, (wide, narrow), lambda c, i: work.add(*c, part_ref, i))
    wide_ref[...], narrow_ref[...], picked_ref[...] = wide[:rows], narrow[:rows], picked
    parcel_ref[0, : work.vectors, :] = gathered_sum(wide[rows:], narrow[rows:])
    parcel_ref[0, work.vectors :, :] = jnp.zeros((work.dims, rows), F32)
    parcel_ref[1] = picked


def middle_body(
    layout, place, side_ref, own_ref, part_ref, wide_in, narrow_in, picked_in,
    wide_ref, narrow_ref, picked_ref,
):
    work = Gathered(*layout, side_ref, own_ref)
    blocks = part_ref.shape[0]
    picked_ref[...] = over(
        blocks, PICK, picked_in[...], lambda c, i: work.pick(c, part_ref, i, place, 0)
    )
    wide_ref[...], narrow_ref[...] = over(
        blocks, CHUNK, (wide_in[...], narrow_in[...]), lambda c, i: work.add(*c, part_ref, i)
    )


def last_body(
    layout, side_ref, own_ref, there_ref, wide_ref, narrow_ref, picked_ref,
    panel_ref, product_ref, rows_ref, total_ref, sems, total_sem,
):
    work = Gathered(*layout, side_ref, own_ref)
    blocks = there_ref.shape[0] - 2
    picked = over(
        blocks,
        PICK,
        picked_ref[...] + there_ref[blocks + 1],
        lambda c, i: work.pick(c, there_ref, i, blocks, 1),
    )
    dims = work.dims
    pivot_x = (picked[:dims] + picked[dims : 2 * dims] + picked[2 * dims :]) * work.scale
    size = pivot_x.shape[1]
    left_pivot = left_stack(pivot_x).T.astype(BF16)
    both = jnp.concatenate([right_stack(pivot_x), right_stack(work.own)], 1)
    values = matern(jnp.dot(left_pivot, both, preferred_element_type=F32))
    eye = lax.broadcasted_iota(jnp.int32, (size, size), 0) == lax.broadcasted_iota(
        jnp.int32, (size, size), 1
    )
    inner = values[:, :size] + jnp.where(eye, work.noise, 0.0)
    a = [inner[i : i + 8] for i in range(0, size, 8)]
    b = [values[i : i + 8, size:] for i in range(0, size, 8)]

    wide, narrow = wide_ref[...], narrow_ref[...]
    wide, narrow = over(blocks, CHUNK, (wide, narrow), lambda c, i: work.add(*c, there_ref, i))
    total = gathered_sum(wide, narrow) + there_ref[blocks, : work.vectors, :]
    total_ref[...] = total + work.noise * own_ref[dims:, :]
    steps = size // BLOCK
    copies = []
    for step in range(steps):
        rows = pl.ds(step * BLOCK, BLOCK)
        rows_ref[rows, :] = eliminate(a, b, step)
        copies.append(
            pltpu.make_async_copy(rows_ref.at[rows, :], panel_ref.at[rows, :], sems.at[step])
        )
        copies[-1].start()
        if step == steps // 2:
            copies.append(pltpu.make_async_copy(total_ref, product_ref, total_sem))
            copies[-1].start()
    for copy in copies:
        copy.wait()


VMEM = pl.BlockSpec(memory_space=pltpu.VMEM)
PARAMS = pltpu.CompilerParams(vmem_limit_bytes=32 * 1024 * 1024)


def cost(points, rows):
    return pl.CostEstimate(
        flops=points * rows * 60, bytes_accessed=points * 100, transcendentals=points * rows * 2
    )


def sums(side, own):
    rows, vectors = own.shape[1], own.shape[0] - side.shape[0] + 2
    return (
        jax.ShapeDtypeStruct((rows, 2 * vectors), F32),
        jax.ShapeDtypeStruct((rows, vectors), F32),
        jax.ShapeDtypeStruct((3 * (side.shape[0] - 2), side.shape[1]), F32),
    )


def early(layout, side, own, mate, part):
    rows = own.shape[1]
    return pl.pallas_call(
        functools.partial(early_body, layout),
        out_shape=sums(side, own) + (jax.ShapeDtypeStruct((2,) + own.shape, F32),),
        in_specs=[VMEM] * 4,
        out_specs=(VMEM,) * 4,
        cost_estimate=cost(part.shape[0] * rows, 2 * rows),
        compiler_params=PARAMS,
    )(side, own, mate, part)


def middle(layout, place, side, own, part, *carry):
    rows = own.shape[1]
    return pl.pallas_call(
        functools.partial(middle_body, layout, place),
        out_shape=sums(side, own),
        in_specs=[VMEM] * 6,
        out_specs=(VMEM,) * 3,
        cost_estimate=cost(part.shape[0] * rows, rows),
        compiler_params=PARAMS,
    )(side, own, part, *carry)


def finish(layout, side, own, there, *carry):
    size, rows = side.shape[1], own.shape[1]
    product = (own.shape[0] - side.shape[0] + 2, rows)
    return pl.pallas_call(
        functools.partial(last_body, layout),
        out_shape=(
            jax.ShapeDtypeStruct((size, rows), F32),
            jax.ShapeDtypeStruct(product, F32),
        ),
        in_specs=[VMEM] * (3 + len(carry)),
        out_specs=(pl.BlockSpec(memory_space=pl.ANY),) * 2,
        scratch_shapes=[
            pltpu.VMEM((size, rows), F32),
            pltpu.VMEM(product, F32),
            pltpu.SemaphoreType.DMA((size // BLOCK,)),
            pltpu.SemaphoreType.DMA,
        ],
        compiler_params=PARAMS,
    )(side, own, there, *carry)


def solution(mesh):
    groups, members = mesh.shape["blk"], mesh.shape["grp"]
    count = groups * members
    masks = exchange_masks(groups, members)

    def swap(value, step):
        pairs = [(i, i ^ masks[parity(i, count)][step]) for i in range(count)]
        return lax.ppermute(value, ("blk", "grp"), pairs)

    def local(inputs, probes, lengths, noise, pivots):
        rows = inputs.shape[1]
        layout = (masks, count, members)
        last = len(masks[0]) - 1
        own = jnp.concatenate([inputs, probes], 0)
        came = [swap(inputs, 0), swap(probes, 0)]
        here = jnp.stack([own, jnp.concatenate(came, 0)])
        side = jnp.concatenate(
            [
                jnp.broadcast_to((SCALE / lengths)[:, None], inputs.shape),
                jnp.broadcast_to(noise[:, None], (1, rows)),
                pivots.astype(F32)[None, :],
            ],
            0,
        )
        for step in range(1, last - 1):
            here = jnp.concatenate([here, swap(here, step)], 0)
            if step == 1:
                mate = swap(lax.optimization_barrier((own, here))[0], last)
        arrived = swap(here, last - 1)
        *carry, parcel = early(layout, side, own, mate, here)
        arrived, parcel = lax.optimization_barrier((arrived, parcel))
        there = swap(jnp.concatenate([arrived, parcel], 0), last)
        carry = middle(layout, here.shape[0], side, own, arrived, *carry)
        return finish(layout, side, own, there, *carry)

    in_specs = (P(None, ("blk", "grp")), P(None, ("blk", "grp")), P(), P(), P())
    out_specs = (P(None, ("blk", "grp")), P(None, ("blk", "grp")))
    return jax.shard_map(local, mesh=mesh, in_specs=in_specs, out_specs=out_specs, check_vma=False)
```

```python
import functools
import math

import jax
import jax.numpy as jnp
from jax import lax
from jax.experimental import pallas as pl
from jax.experimental.pallas import tpu as pltpu
from jax.sharding import PartitionSpec as P

F32 = jnp.float32
BF16 = jnp.bfloat16
LN2 = math.log(2.0)
SCALE = math.sqrt(5.0) / LN2
BLOCK = 16
CHUNK = 4
PICK = 2
UNROLL = 32


def exchange_masks(groups, members):
    low = members.bit_length() - 1
    bits = [1 << bit for bit in range(low - 1, 1, -1)]
    bits += [1 << (low + bit) for bit in range(groups.bit_length() - 2, -1, -1)]
    bits += [2] if members > 2 else []
    even = [bit | 1 for bit in bits]
    odd = even[:-2] + even[:-3:-1]
    return even + [1], odd + [1]


def parity(index, count):
    bits = 0
    for bit in range(count.bit_length() - 1):
        bits = bits ^ (index >> bit)
    return bits & 1


def split3(value):
    high = value.astype(BF16).astype(F32)
    rest = value - high
    middle = rest.astype(BF16).astype(F32)
    return high, middle, rest - middle


def norm_tile(x, first):
    high, middle, low = split3(jnp.sum(x * x, axis=0, keepdims=True))
    row = lax.broadcasted_iota(jnp.int32, x.shape, 0)
    if not first:
        row = jnp.where(row < 3, row + 3, row - 3)
    tile = jnp.where(row < 6, 1.0, 0.0)
    tile = jnp.where(row == 0, high, tile)
    tile = jnp.where(row == 1, middle, tile)
    return jnp.where(row == 2, low, tile)


def left_stack(x):
    high, middle, low = split3(x)
    return jnp.concatenate(
        [high, high, high, middle, middle, low, norm_tile(x, True), jnp.zeros_like(x)], 0
    )


def right_stack(x):
    high, middle, low = split3(-2.0 * x)
    return jnp.concatenate(
        [high, middle, low, high, middle, high, norm_tile(x, False), jnp.zeros_like(x)], 0
    ).astype(BF16)


def matern(square):
    square = jnp.maximum(square, 1e-30)
    radius = square * lax.rsqrt(square)
    return (1.0 + LN2 * radius + (LN2 * LN2 / 3.0) * square) * jnp.exp2(-radius)


def rows_of(value, row):
    return jnp.broadcast_to(value[row : row + 1, :], value.shape)


def eliminate(a, b, step):
    tiles = BLOCK // 8
    base, first = step * BLOCK, step * tiles
    later = first + 2 * tiles
    sub = lax.broadcasted_iota(jnp.int32, (8, 128), 0)

    def column(piece, m):
        return jnp.broadcast_to(piece[:, base + m : base + m + 1], (8, 128))

    ra, rb = a[first : first + tiles], b[first : first + tiles]
    cols = [[column(piece, m) for piece in ra] for m in range(BLOCK)]
    below = [[column(piece, m) for piece in a[first + tiles : later]] for m in range(BLOCK)]
    if later < len(a):
        l_high, l_middle, l_low = [
            part.astype(BF16) for part in split3(jnp.concatenate(a[later:], 0))
        ]
        left = jnp.concatenate([l_high, l_middle], 1)
    out = [jnp.zeros((8, 128), F32) for t in range(tiles)]
    for j in range(0, BLOCK, 2):
        v, s = divmod(j, 8)
        one, two = cols[j], cols[j + 1]
        top, side, end = rows_of(one[v], s), rows_of(one[v], s + 1), rows_of(two[v], s + 1)
        det = top * end - side * side
        inverse = 1.0 / det
        row_a, next_a = rows_of(ra[v], s), rows_of(ra[v], s + 1)
        row_b, next_b = rows_of(rb[v], s), rows_of(rb[v], s + 1)
        root = lax.rsqrt(top)
        out[v] = jnp.where(sub == s, row_b * root, out[v])
        out[v] = jnp.where(
            sub == s + 1, (top * next_b - side * row_b) * (root * lax.rsqrt(det)), out[v]
        )
        one, two = list(one), list(two)
        one[v] = one[v] - jnp.where(sub == s, 1.0, 0.0)
        two[v] = two[v] - jnp.where(sub == s + 1, 1.0, 0.0)
        first_coef = [(x * end - y * side) * inverse for x, y in zip(one, two)]
        next_coef = [(y * top - x * side) * inverse for x, y in zip(one, two)]
        for t in range(tiles):
            ra[t] = ra[t] - first_coef[t] * row_a - next_coef[t] * next_a
            rb[t] = rb[t] - first_coef[t] * row_b - next_coef[t] * next_b
        for m in range(j + 2, BLOCK):
            entry, following = rows_of(cols[m][v], s), rows_of(cols[m][v], s + 1)
            for t in range(tiles):
                change = first_coef[t] * entry + next_coef[t] * following
                cols[m][t] = cols[m][t] - change
    if first + tiles < len(a):
        for values, rows in ((a, ra), (b, rb)):
            sums = [[None, None] for u in range(tiles)]
            for j in range(BLOCK):
                row = rows_of(rows[j // 8], j % 8)
                for u in range(tiles):
                    term = below[j][u] * row
                    before = sums[u][j % 2]
                    sums[u][j % 2] = term if before is None else before + term
            for u in range(tiles):
                at = first + tiles + u
                values[at] = values[at] - (sums[u][0] + sums[u][1])
    if later < len(a):
        solved = jnp.concatenate([jnp.concatenate(ra, 0), jnp.concatenate(rb, 0)], 1)

        def placed(value):
            parts = [value.astype(BF16)]
            if base:
                parts.insert(0, jnp.zeros((base, value.shape[1]), BF16))
            parts.append(jnp.zeros((8 * len(a) - base - BLOCK, value.shape[1]), BF16))
            return jnp.concatenate(parts, 0)

        w_high, w_middle, w_low = [placed(part) for part in split3(solved)]
        change = (
            jnp.dot(left, jnp.concatenate([w_high, w_high], 0), preferred_element_type=F32)
            + jnp.dot(left, jnp.concatenate([w_middle, w_middle], 0), preferred_element_type=F32)
            + jnp.dot(
                jnp.concatenate([l_high, l_low], 1),
                jnp.concatenate([w_low, w_high], 0),
                preferred_element_type=F32,
            )
        )
        for t in range(later, len(a)):
            rows = slice(8 * (t - later), 8 * (t - later) + 8)
            a[t] = a[t] - change[rows, :128]
            b[t] = b[t] - change[rows, 128:]
    return jnp.concatenate(out, 0)


NT = (((1,), (1,)), ((), ()))


class Gathered:
    def __init__(self, masks, count, members, side_ref, own_ref, *mate_refs):
        self.masks, self.count = masks, count
        self.me = lax.axis_index("blk") * members + lax.axis_index("grp")
        self.kind = parity(self.me, count)
        self.rows = own_ref.shape[1]
        self.dims = side_ref.shape[0] - 2
        self.vectors = own_ref.shape[0] - self.dims
        self.scale = side_ref[: self.dims, :]
        self.noise = side_ref[self.dims : self.dims + 1, :]
        self.pivots = side_ref[self.dims + 1 : self.dims + 2, :].astype(jnp.int32)
        self.points = lax.broadcasted_iota(jnp.int32, (self.rows, self.pivots.shape[1]), 0)
        self.own = own_ref[: self.dims, :] * self.scale
        lefts = [left_stack(self.own)]
        lefts += [left_stack(ref[: self.dims, :] * self.scale) for ref in mate_refs]
        self.left_own = jnp.concatenate([left.T.astype(BF16) for left in lefts], 0)

    def start(self):
        wide = jnp.zeros((self.left_own.shape[0], 2 * self.vectors), F32)
        narrow = jnp.zeros((self.left_own.shape[0], self.vectors), F32)
        return wide, narrow, jnp.zeros((3 * self.dims, self.pivots.shape[1]), F32)

    def owner(self, index, other):
        device, kind = self.me ^ other, self.kind ^ other
        for bit, (even, odd) in enumerate(zip(self.masks[0][:-1], self.masks[1][:-1])):
            device = device ^ (((index >> bit) & 1) * jnp.where(kind == 0, even, odd))
        return device

    def pick(self, total, ref, index, place, other):
        hots, parts = [], []
        for i in range(PICK):
            device = self.owner(place + index + i, other)
            hots.append((self.points == self.pivots - device * self.rows).astype(F32).astype(BF16))
            parts.append(jnp.concatenate(split3(ref[index + i, : self.dims, :]), 0).astype(BF16))
        return total + jnp.dot(
            jnp.concatenate(parts, 1), jnp.concatenate(hots, 0), preferred_element_type=F32
        )

    def add(self, wide, narrow, ref, index):
        blocks = [ref[index + i] for i in range(CHUNK)]
        right = jnp.concatenate(
            [right_stack(block[: self.dims] * self.scale) for block in blocks], 1
        )
        probe = jnp.concatenate([block[self.dims :] for block in blocks], 1)
        probe_high = probe.astype(BF16)
        probe_low = (probe - probe_high.astype(F32)).astype(BF16)
        value = matern(jnp.dot(self.left_own, right, preferred_element_type=F32))
        value_high = value.astype(BF16)
        value_low = (value - value_high.astype(F32)).astype(BF16)
        both = jnp.concatenate([probe_high, probe_low], 0)
        wide = wide + lax.dot_general(value_high, both, NT, preferred_element_type=F32)
        narrow = narrow + lax.dot_general(value_low, probe_high, NT, preferred_element_type=F32)
        return wide, narrow


def over(blocks, width, carry, visit):
    steps = blocks // width
    if blocks <= UNROLL:
        for i in range(steps):
            carry = visit(carry, i * width)
        return carry
    return lax.fori_loop(0, steps, lambda i, c: visit(c, i * width), carry)


def gathered_sum(wide, narrow):
    vectors = narrow.shape[1]
    return (wide[:, :vectors] + wide[:, vectors:] + narrow).T


def early_body(layout, side_ref, own_ref, mate_ref, part_ref, wide_ref, narrow_ref, picked_ref, parcel_ref):
    work = Gathered(*layout, side_ref, own_ref, mate_ref)
    wide, narrow, picked = work.start()
    blocks, rows = part_ref.shape[0], work.rows
    picked = over(blocks, PICK, picked, lambda c, i: work.pick(c, part_ref, i, 0, 0))
    wide, narrow = over(blocks, CHUNK, (wide, narrow), lambda c, i: work.add(*c, part_ref, i))
    wide_ref[...], narrow_ref[...], picked_ref[...] = wide[:rows], narrow[:rows], picked
    parcel_ref[0, : work.vectors, :] = gathered_sum(wide[rows:], narrow[rows:])
    parcel_ref[0, work.vectors :, :] = jnp.zeros((work.dims, rows), F32)
    parcel_ref[1] = picked


def middle_body(
    layout, place, side_ref, own_ref, part_ref, wide_in, narrow_in, picked_in,
    wide_ref, narrow_ref, picked_ref,
):
    work = Gathered(*layout, side_ref, own_ref)
    blocks = part_ref.shape[0]
    picked_ref[...] = over(
        blocks, PICK, picked_in[...], lambda c, i: work.pick(c, part_ref, i, place, 0)
    )
    wide_ref[...], narrow_ref[...] = over(
        blocks, CHUNK, (wide_in[...], narrow_in[...]), lambda c, i: work.add(*c, part_ref, i)
    )


def last_body(
    layout, side_ref, own_ref, there_ref, wide_ref, narrow_ref, picked_ref,
    panel_ref, product_ref, rows_ref, total_ref, sems, total_sem,
):
    work = Gathered(*layout, side_ref, own_ref)
    blocks = there_ref.shape[0] - 2
    picked = over(
        blocks,
        PICK,
        picked_ref[...] + there_ref[blocks + 1],
        lambda c, i: work.pick(c, there_ref, i, blocks, 1),
    )
    dims = work.dims
    pivot_x = (picked[:dims] + picked[dims : 2 * dims] + picked[2 * dims :]) * work.scale
    size = pivot_x.shape[1]
    left_pivot = left_stack(pivot_x).T.astype(BF16)
    both = jnp.concatenate([right_stack(pivot_x), right_stack(work.own)], 1)
    values = matern(jnp.dot(left_pivot, both, preferred_element_type=F32))
    eye = lax.broadcasted_iota(jnp.int32, (size, size), 0) == lax.broadcasted_iota(
        jnp.int32, (size, size), 1
    )
    inner = values[:, :size] + jnp.where(eye, work.noise, 0.0)
    a = [inner[i : i + 8] for i in range(0, size, 8)]
    b = [values[i : i + 8, size:] for i in range(0, size, 8)]

    wide, narrow = wide_ref[...], narrow_ref[...]
    wide, narrow = over(blocks, CHUNK, (wide, narrow), lambda c, i: work.add(*c, there_ref, i))
    total = gathered_sum(wide, narrow) + there_ref[blocks, : work.vectors, :]
    total_ref[...] = total + work.noise * own_ref[dims:, :]
    steps = size // BLOCK
    copies = []
    for step in range(steps):
        rows = pl.ds(step * BLOCK, BLOCK)
        rows_ref[rows, :] = eliminate(a, b, step)
        copies.append(
            pltpu.make_async_copy(rows_ref.at[rows, :], panel_ref.at[rows, :], sems.at[step])
        )
        copies[-1].start()
        if step == steps // 2:
            copies.append(pltpu.make_async_copy(total_ref, product_ref, total_sem))
            copies[-1].start()
    for copy in copies:
        copy.wait()


VMEM = pl.BlockSpec(memory_space=pltpu.VMEM)
PARAMS = pltpu.CompilerParams(vmem_limit_bytes=32 * 1024 * 1024)


def cost(points, rows):
    return pl.CostEstimate(
        flops=points * rows * 60, bytes_accessed=points * 100, transcendentals=points * rows * 2
    )


def sums(side, own):
    rows, vectors = own.shape[1], own.shape[0] - side.shape[0] + 2
    return (
        jax.ShapeDtypeStruct((rows, 2 * vectors), F32),
        jax.ShapeDtypeStruct((rows, vectors), F32),
        jax.ShapeDtypeStruct((3 * (side.shape[0] - 2), side.shape[1]), F32),
    )


def early(layout, side, own, mate, part):
    rows = own.shape[1]
    return pl.pallas_call(
        functools.partial(early_body, layout),
        out_shape=sums(side, own) + (jax.ShapeDtypeStruct((2,) + own.shape, F32),),
        in_specs=[VMEM] * 4,
        out_specs=(VMEM,) * 4,
        cost_estimate=cost(part.shape[0] * rows, 2 * rows),
        compiler_params=PARAMS,
    )(side, own, mate, part)


def middle(layout, place, side, own, part, *carry):
    rows = own.shape[1]
    return pl.pallas_call(
        functools.partial(middle_body, layout, place),
        out_shape=sums(side, own),
        in_specs=[VMEM] * 6,
        out_specs=(VMEM,) * 3,
        cost_estimate=cost(part.shape[0] * rows, rows),
        compiler_params=PARAMS,
    )(side, own, part, *carry)


def finish(layout, side, own, there, *carry):
    size, rows = side.shape[1], own.shape[1]
    product = (own.shape[0] - side.shape[0] + 2, rows)
    return pl.pallas_call(
        functools.partial(last_body, layout),
        out_shape=(
            jax.ShapeDtypeStruct((size, rows), F32),
            jax.ShapeDtypeStruct(product, F32),
        ),
        in_specs=[VMEM] * (3 + len(carry)),
        out_specs=(pl.BlockSpec(memory_space=pl.ANY),) * 2,
        scratch_shapes=[
            pltpu.VMEM((size, rows), F32),
            pltpu.VMEM(product, F32),
            pltpu.SemaphoreType.DMA((size // BLOCK,)),
            pltpu.SemaphoreType.DMA,
        ],
        compiler_params=PARAMS,
    )(side, own, there, *carry)


def solution(mesh):
    groups, members = mesh.shape["blk"], mesh.shape["grp"]
    count = groups * members
    masks = exchange_masks(groups, members)

    def swap(value, step):
        pairs = [(i, i ^ masks[parity(i, count)][step]) for i in range(count)]
        return lax.ppermute(value, ("blk", "grp"), pairs)

    def local(inputs, probes, lengths, noise, pivots):
        rows = inputs.shape[1]
        own = jnp.concatenate([inputs, probes], 0)
        layout = (masks, count, members)
        last = len(masks[0]) - 1
        here = own[None]
        for step in range(last - 1):
            if step == 1:
                side = jnp.concatenate(
                    [
                        jnp.broadcast_to((SCALE / lengths)[:, None], inputs.shape),
                        jnp.broadcast_to(noise[:, None], (1, rows)),
                        pivots.astype(F32)[None, :],
                    ],
                    0,
                )
            if step == 1:
                mate = swap(lax.optimization_barrier((own, here))[0], last)
            here = jnp.concatenate([here, swap(here, step)], 0)
        arrived = swap(here, last - 1)
        *carry, parcel = early(layout, side, own, mate, here)
        arrived, parcel = lax.optimization_barrier((arrived, parcel))
        there = swap(jnp.concatenate([arrived, parcel], 0), last)
        carry = middle(layout, here.shape[0], side, own, arrived, *carry)
        return finish(layout, side, own, there, *carry)

    in_specs = (P(None, ("blk", "grp")), P(None, ("blk", "grp")), P(), P(), P())
    out_specs = (P(None, ("blk", "grp")), P(None, ("blk", "grp")))
    return jax.shard_map(local, mesh=mesh, in_specs=in_specs, out_specs=out_specs, check_vma=False)
```

```python
import functools
import math

import jax
import jax.numpy as jnp
from jax import lax
from jax.experimental import pallas as pl
from jax.experimental.pallas import tpu as pltpu
from jax.sharding import PartitionSpec as P

F32 = jnp.float32
BF16 = jnp.bfloat16
LN2 = math.log(2.0)
SCALE = math.sqrt(5.0) / LN2
BLOCK = 16
CHUNK = 8
PICK = 4
UNROLL = 32


def exchange_masks(groups, members):
    low = members.bit_length() - 1
    bits = [1 << bit for bit in range(low - 1, 1, -1)]
    bits += [1 << (low + bit) for bit in range(groups.bit_length() - 2, -1, -1)]
    bits += [2] if members > 2 else []
    even = [bit | 1 for bit in bits]
    odd = even[:-2] + even[:-3:-1]
    return even + [1], odd + [1]


def parity(index, count):
    bits = 0
    for bit in range(count.bit_length() - 1):
        bits = bits ^ (index >> bit)
    return bits & 1


def split3(value):
    high = value.astype(BF16).astype(F32)
    rest = value - high
    middle = rest.astype(BF16).astype(F32)
    return high, middle, rest - middle


def norm_tile(x, first):
    high, middle, low = split3(jnp.sum(x * x, axis=0, keepdims=True))
    row = lax.broadcasted_iota(jnp.int32, x.shape, 0)
    if not first:
        row = jnp.where(row < 3, row + 3, row - 3)
    tile = jnp.where(row < 6, 1.0, 0.0)
    tile = jnp.where(row == 0, high, tile)
    tile = jnp.where(row == 1, middle, tile)
    return jnp.where(row == 2, low, tile)


def left_stack(x):
    high, middle, low = split3(x)
    return jnp.concatenate(
        [high, high, high, middle, middle, low, norm_tile(x, True), jnp.zeros_like(x)], 0
    )


def right_stack(x):
    high, middle, low = split3(-2.0 * x)
    return jnp.concatenate(
        [high, middle, low, high, middle, high, norm_tile(x, False), jnp.zeros_like(x)], 0
    ).astype(BF16)


def matern(square):
    square = jnp.maximum(square, 1e-30)
    radius = square * lax.rsqrt(square)
    return (1.0 + LN2 * radius + (LN2 * LN2 / 3.0) * square) * jnp.exp2(-radius)


def rows_of(value, row):
    return jnp.broadcast_to(value[row : row + 1, :], value.shape)


def eliminate(a, b, step):
    tiles = BLOCK // 8
    base, first = step * BLOCK, step * tiles
    later = first + 2 * tiles
    sub = lax.broadcasted_iota(jnp.int32, (8, 128), 0)

    def column(piece, m):
        return jnp.broadcast_to(piece[:, base + m : base + m + 1], (8, 128))

    ra, rb = a[first : first + tiles], b[first : first + tiles]
    cols = [[column(piece, m) for piece in ra] for m in range(BLOCK)]
    below = [[column(piece, m) for piece in a[first + tiles : later]] for m in range(BLOCK)]
    if later < len(a):
        l_high, l_middle, l_low = [
            part.astype(BF16) for part in split3(jnp.concatenate(a[later:], 0))
        ]
        left = jnp.concatenate([l_high, l_middle], 1)
    out = [jnp.zeros((8, 128), F32) for t in range(tiles)]
    for j in range(0, BLOCK, 2):
        v, s = divmod(j, 8)
        one, two = cols[j], cols[j + 1]
        top, side, end = rows_of(one[v], s), rows_of(one[v], s + 1), rows_of(two[v], s + 1)
        det = top * end - side * side
        inverse = 1.0 / det
        row_a, next_a = rows_of(ra[v], s), rows_of(ra[v], s + 1)
        row_b, next_b = rows_of(rb[v], s), rows_of(rb[v], s + 1)
        root = lax.rsqrt(top)
        out[v] = jnp.where(sub == s, row_b * root, out[v])
        out[v] = jnp.where(
            sub == s + 1, (top * next_b - side * row_b) * (root * lax.rsqrt(det)), out[v]
        )
        one, two = list(one), list(two)
        one[v] = one[v] - jnp.where(sub == s, 1.0, 0.0)
        two[v] = two[v] - jnp.where(sub == s + 1, 1.0, 0.0)
        first_coef = [(x * end - y * side) * inverse for x, y in zip(one, two)]
        next_coef = [(y * top - x * side) * inverse for x, y in zip(one, two)]
        for t in range(tiles):
            ra[t] = ra[t] - first_coef[t] * row_a - next_coef[t] * next_a
            rb[t] = rb[t] - first_coef[t] * row_b - next_coef[t] * next_b
        for m in range(j + 2, BLOCK):
            entry, following = rows_of(cols[m][v], s), rows_of(cols[m][v], s + 1)
            for t in range(tiles):
                change = first_coef[t] * entry + next_coef[t] * following
                cols[m][t] = cols[m][t] - change
    if first + tiles < len(a):
        for values, rows in ((a, ra), (b, rb)):
            for j in range(BLOCK):
                row = rows_of(rows[j // 8], j % 8)
                for u in range(tiles):
                    at = first + tiles + u
                    values[at] = values[at] - below[j][u] * row
    if later < len(a):
        solved = jnp.concatenate([jnp.concatenate(ra, 0), jnp.concatenate(rb, 0)], 1)

        def placed(value):
            parts = [value.astype(BF16)]
            if base:
                parts.insert(0, jnp.zeros((base, value.shape[1]), BF16))
            parts.append(jnp.zeros((8 * len(a) - base - BLOCK, value.shape[1]), BF16))
            return jnp.concatenate(parts, 0)

        w_high, w_middle, w_low = [placed(part) for part in split3(solved)]
        change = (
            jnp.dot(left, jnp.concatenate([w_high, w_high], 0), preferred_element_type=F32)
            + jnp.dot(left, jnp.concatenate([w_middle, w_middle], 0), preferred_element_type=F32)
            + jnp.dot(
                jnp.concatenate([l_high, l_low], 1),
                jnp.concatenate([w_low, w_high], 0),
                preferred_element_type=F32,
            )
        )
        for t in range(later, len(a)):
            rows = slice(8 * (t - later), 8 * (t - later) + 8)
            a[t] = a[t] - change[rows, :128]
            b[t] = b[t] - change[rows, 128:]
    return jnp.concatenate(out, 0)


NT = (((1,), (1,)), ((), ()))


class Gathered:
    def __init__(self, masks, count, members, side_ref, own_ref, *mate_refs):
        self.masks, self.count = masks, count
        self.me = lax.axis_index("blk") * members + lax.axis_index("grp")
        self.kind = parity(self.me, count)
        self.rows = own_ref.shape[1]
        self.dims = side_ref.shape[0] - 2
        self.vectors = own_ref.shape[0] - self.dims
        self.scale = side_ref[: self.dims, :]
        self.noise = side_ref[self.dims : self.dims + 1, :]
        self.pivots = side_ref[self.dims + 1 : self.dims + 2, :].astype(jnp.int32)
        self.points = lax.broadcasted_iota(jnp.int32, (self.rows, self.pivots.shape[1]), 0)
        self.own = own_ref[: self.dims, :] * self.scale
        lefts = [left_stack(self.own)]
        lefts += [left_stack(ref[: self.dims, :] * self.scale) for ref in mate_refs]
        self.left_own = jnp.concatenate([left.T.astype(BF16) for left in lefts], 0)

    def start(self):
        wide = jnp.zeros((self.left_own.shape[0], 2 * self.vectors), F32)
        narrow = jnp.zeros((self.left_own.shape[0], self.vectors), F32)
        return wide, narrow, jnp.zeros((3 * self.dims, self.pivots.shape[1]), F32)

    def owner(self, index, other):
        device, kind = self.me ^ other, self.kind ^ other
        for bit, (even, odd) in enumerate(zip(self.masks[0][:-1], self.masks[1][:-1])):
            device = device ^ (((index >> bit) & 1) * jnp.where(kind == 0, even, odd))
        return device

    def pick(self, total, ref, index, place, other):
        hots, parts = [], []
        for i in range(PICK):
            device = self.owner(place + index + i, other)
            hots.append((self.points == self.pivots - device * self.rows).astype(F32).astype(BF16))
            parts.append(jnp.concatenate(split3(ref[index + i, : self.dims, :]), 0).astype(BF16))
        return total + jnp.dot(
            jnp.concatenate(parts, 1), jnp.concatenate(hots, 0), preferred_element_type=F32
        )

    def add(self, wide, narrow, ref, index):
        blocks = [ref[index + i] for i in range(CHUNK)]
        right = jnp.concatenate(
            [right_stack(block[: self.dims] * self.scale) for block in blocks], 1
        )
        probe = jnp.concatenate([block[self.dims :] for block in blocks], 1)
        probe_high = probe.astype(BF16)
        probe_low = (probe - probe_high.astype(F32)).astype(BF16)
        value = matern(jnp.dot(self.left_own, right, preferred_element_type=F32))
        value_high = value.astype(BF16)
        value_low = (value - value_high.astype(F32)).astype(BF16)
        both = jnp.concatenate([probe_high, probe_low], 0)
        wide = wide + lax.dot_general(value_high, both, NT, preferred_element_type=F32)
        narrow = narrow + lax.dot_general(value_low, probe_high, NT, preferred_element_type=F32)
        return wide, narrow


def over(blocks, width, carry, visit):
    steps = blocks // width
    if blocks <= UNROLL:
        for i in range(steps):
            carry = visit(carry, i * width)
        return carry
    return lax.fori_loop(0, steps, lambda i, c: visit(c, i * width), carry)


def gathered_sum(wide, narrow):
    vectors = narrow.shape[1]
    return (wide[:, :vectors] + wide[:, vectors:] + narrow).T


def early_body(layout, side_ref, own_ref, mate_ref, part_ref, wide_ref, narrow_ref, picked_ref, parcel_ref):
    work = Gathered(*layout, side_ref, own_ref, mate_ref)
    wide, narrow, picked = work.start()
    blocks, rows = part_ref.shape[0], work.rows
    picked = over(blocks, PICK, picked, lambda c, i: work.pick(c, part_ref, i, 0, 0))
    wide, narrow = over(blocks, CHUNK, (wide, narrow), lambda c, i: work.add(*c, part_ref, i))
    wide_ref[...], narrow_ref[...], picked_ref[...] = wide[:rows], narrow[:rows], picked
    parcel_ref[0, : work.vectors, :] = gathered_sum(wide[rows:], narrow[rows:])
    parcel_ref[0, work.vectors :, :] = jnp.zeros((work.dims, rows), F32)
    parcel_ref[1] = picked


def middle_body(
    layout, place, side_ref, own_ref, part_ref, wide_in, narrow_in, picked_in,
    wide_ref, narrow_ref, picked_ref,
):
    work = Gathered(*layout, side_ref, own_ref)
    blocks = part_ref.shape[0]
    picked_ref[...] = over(
        blocks, PICK, picked_in[...], lambda c, i: work.pick(c, part_ref, i, place, 0)
    )
    wide_ref[...], narrow_ref[...] = over(
        blocks, CHUNK, (wide_in[...], narrow_in[...]), lambda c, i: work.add(*c, part_ref, i)
    )


def last_body(
    layout, side_ref, own_ref, there_ref, wide_ref, narrow_ref, picked_ref,
    panel_ref, product_ref, rows_ref, total_ref, sems, total_sem,
):
    work = Gathered(*layout, side_ref, own_ref)
    blocks = there_ref.shape[0] - 2
    picked = over(
        blocks,
        PICK,
        picked_ref[...] + there_ref[blocks + 1],
        lambda c, i: work.pick(c, there_ref, i, blocks, 1),
    )
    dims = work.dims
    pivot_x = (picked[:dims] + picked[dims : 2 * dims] + picked[2 * dims :]) * work.scale
    size = pivot_x.shape[1]
    left_pivot = left_stack(pivot_x).T.astype(BF16)
    both = jnp.concatenate([right_stack(pivot_x), right_stack(work.own)], 1)
    values = matern(jnp.dot(left_pivot, both, preferred_element_type=F32))
    eye = lax.broadcasted_iota(jnp.int32, (size, size), 0) == lax.broadcasted_iota(
        jnp.int32, (size, size), 1
    )
    inner = values[:, :size] + jnp.where(eye, work.noise, 0.0)
    a = [inner[i : i + 8] for i in range(0, size, 8)]
    b = [values[i : i + 8, size:] for i in range(0, size, 8)]

    wide, narrow = wide_ref[...], narrow_ref[...]
    wide, narrow = over(blocks, CHUNK, (wide, narrow), lambda c, i: work.add(*c, there_ref, i))
    total = gathered_sum(wide, narrow) + there_ref[blocks, : work.vectors, :]
    total_ref[...] = total + work.noise * own_ref[dims:, :]
    steps = size // BLOCK
    copies = []
    for step in range(steps):
        rows = pl.ds(step * BLOCK, BLOCK)
        rows_ref[rows, :] = eliminate(a, b, step)
        copies.append(
            pltpu.make_async_copy(rows_ref.at[rows, :], panel_ref.at[rows, :], sems.at[step])
        )
        copies[-1].start()
        if step == steps // 2:
            copies.append(pltpu.make_async_copy(total_ref, product_ref, total_sem))
            copies[-1].start()
    for copy in copies:
        copy.wait()


VMEM = pl.BlockSpec(memory_space=pltpu.VMEM)
PARAMS = pltpu.CompilerParams(vmem_limit_bytes=32 * 1024 * 1024)


def cost(points, rows):
    return pl.CostEstimate(
        flops=points * rows * 60, bytes_accessed=points * 100, transcendentals=points * rows * 2
    )


def sums(side, own):
    rows, vectors = own.shape[1], own.shape[0] - side.shape[0] + 2
    return (
        jax.ShapeDtypeStruct((rows, 2 * vectors), F32),
        jax.ShapeDtypeStruct((rows, vectors), F32),
        jax.ShapeDtypeStruct((3 * (side.shape[0] - 2), side.shape[1]), F32),
    )


def early(layout, side, own, mate, part):
    rows = own.shape[1]
    return pl.pallas_call(
        functools.partial(early_body, layout),
        out_shape=sums(side, own) + (jax.ShapeDtypeStruct((2,) + own.shape, F32),),
        in_specs=[VMEM] * 4,
        out_specs=(VMEM,) * 4,
        cost_estimate=cost(part.shape[0] * rows, 2 * rows),
        compiler_params=PARAMS,
    )(side, own, mate, part)


def middle(layout, place, side, own, part, *carry):
    rows = own.shape[1]
    return pl.pallas_call(
        functools.partial(middle_body, layout, place),
        out_shape=sums(side, own),
        in_specs=[VMEM] * 6,
        out_specs=(VMEM,) * 3,
        cost_estimate=cost(part.shape[0] * rows, rows),
        compiler_params=PARAMS,
    )(side, own, part, *carry)


def finish(layout, side, own, there, *carry):
    size, rows = side.shape[1], own.shape[1]
    product = (own.shape[0] - side.shape[0] + 2, rows)
    return pl.pallas_call(
        functools.partial(last_body, layout),
        out_shape=(
            jax.ShapeDtypeStruct((size, rows), F32),
            jax.ShapeDtypeStruct(product, F32),
        ),
        in_specs=[VMEM] * (3 + len(carry)),
        out_specs=(pl.BlockSpec(memory_space=pl.ANY),) * 2,
        scratch_shapes=[
            pltpu.VMEM((size, rows), F32),
            pltpu.VMEM(product, F32),
            pltpu.SemaphoreType.DMA((size // BLOCK,)),
            pltpu.SemaphoreType.DMA,
        ],
        compiler_params=PARAMS,
    )(side, own, there, *carry)


def solution(mesh):
    groups, members = mesh.shape["blk"], mesh.shape["grp"]
    count = groups * members
    masks = exchange_masks(groups, members)

    def swap(value, step):
        pairs = [(i, i ^ masks[parity(i, count)][step]) for i in range(count)]
        return lax.ppermute(value, ("blk", "grp"), pairs)

    def local(inputs, probes, lengths, noise, pivots):
        rows = inputs.shape[1]
        own = jnp.concatenate([inputs, probes], 0)
        layout = (masks, count, members)
        last = len(masks[0]) - 1
        here = own[None]
        for step in range(last - 1):
            if step == 1:
                side = jnp.concatenate(
                    [
                        jnp.broadcast_to((SCALE / lengths)[:, None], inputs.shape),
                        jnp.broadcast_to(noise[:, None], (1, rows)),
                        pivots.astype(F32)[None, :],
                    ],
                    0,
                )
            if step == 1:
                mate = swap(lax.optimization_barrier((own, here))[0], last)
            here = jnp.concatenate([here, swap(here, step)], 0)
        arrived = swap(here, last - 1)
        *carry, parcel = early(layout, side, own, mate, here)
        arrived, parcel = lax.optimization_barrier((arrived, parcel))
        there = swap(jnp.concatenate([arrived, parcel], 0), last)
        carry = middle(layout, here.shape[0], side, own, arrived, *carry)
        return finish(layout, side, own, there, *carry)

    in_specs = (P(None, ("blk", "grp")), P(None, ("blk", "grp")), P(), P(), P())
    out_specs = (P(None, ("blk", "grp")), P(None, ("blk", "grp")))
    return jax.shard_map(local, mesh=mesh, in_specs=in_specs, out_specs=out_specs, check_vma=False)
```

```python
import functools
import math

import jax
import jax.numpy as jnp
from jax import lax
from jax.experimental import pallas as pl
from jax.experimental.pallas import tpu as pltpu
from jax.sharding import PartitionSpec as P

F32 = jnp.float32
BF16 = jnp.bfloat16
LN2 = math.log(2.0)
SCALE = math.sqrt(5.0) / LN2
BLOCK = 16
CHUNK = 8
PICK = 4
UNROLL = 32


def exchange_masks(groups, members):
    low = members.bit_length() - 1
    bits = [1 << bit for bit in range(low - 1, 1, -1)]
    bits += [1 << (low + bit) for bit in range(groups.bit_length() - 2, -1, -1)]
    bits += [2] if members > 2 else []
    even = [bit | 1 for bit in bits]
    odd = even[:-2] + even[:-3:-1]
    return even + [1], odd + [1]


def parity(index, count):
    bits = 0
    for bit in range(count.bit_length() - 1):
        bits = bits ^ (index >> bit)
    return bits & 1


def split3(value):
    high = value.astype(BF16).astype(F32)
    rest = value - high
    middle = rest.astype(BF16).astype(F32)
    return high, middle, rest - middle


def norm_tile(x, first):
    high, middle, low = split3(jnp.sum(x * x, axis=0, keepdims=True))
    row = lax.broadcasted_iota(jnp.int32, x.shape, 0)
    if not first:
        row = jnp.where(row < 3, row + 3, row - 3)
    tile = jnp.where(row < 6, 1.0, 0.0)
    tile = jnp.where(row == 0, high, tile)
    tile = jnp.where(row == 1, middle, tile)
    return jnp.where(row == 2, low, tile)


def left_stack(x):
    high, middle, low = split3(x)
    return jnp.concatenate(
        [high, high, high, middle, middle, low, norm_tile(x, True), jnp.zeros_like(x)], 0
    )


def right_stack(x):
    high, middle, low = split3(-2.0 * x)
    return jnp.concatenate(
        [high, middle, low, high, middle, high, norm_tile(x, False), jnp.zeros_like(x)], 0
    ).astype(BF16)


def matern(square):
    square = jnp.maximum(square, 1e-30)
    radius = square * lax.rsqrt(square)
    return (1.0 + LN2 * radius + (LN2 * LN2 / 3.0) * square) * jnp.exp2(-radius)


def rows_of(value, row):
    return jnp.broadcast_to(value[row : row + 1, :], value.shape)


def eliminate(a, b, step):
    tiles = BLOCK // 8
    base, first = step * BLOCK, step * tiles
    later = first + 2 * tiles
    sub = lax.broadcasted_iota(jnp.int32, (8, 128), 0)

    def column(piece, m):
        return jnp.broadcast_to(piece[:, base + m : base + m + 1], (8, 128))

    ra, rb = a[first : first + tiles], b[first : first + tiles]
    cols = [[column(piece, m) for piece in ra] for m in range(BLOCK)]
    below = [[column(piece, m) for piece in a[first + tiles : later]] for m in range(BLOCK)]
    if later < len(a):
        l_high, l_middle, l_low = [
            part.astype(BF16) for part in split3(jnp.concatenate(a[later:], 0))
        ]
        left = jnp.concatenate([l_high, l_middle], 1)
    out = [jnp.zeros((8, 128), F32) for t in range(tiles)]
    for j in range(0, BLOCK, 2):
        v, s = divmod(j, 8)
        one, two = cols[j], cols[j + 1]
        top, side, end = rows_of(one[v], s), rows_of(one[v], s + 1), rows_of(two[v], s + 1)
        det = top * end - side * side
        inverse = 1.0 / det
        row_a, next_a = rows_of(ra[v], s), rows_of(ra[v], s + 1)
        row_b, next_b = rows_of(rb[v], s), rows_of(rb[v], s + 1)
        root = lax.rsqrt(top)
        out[v] = jnp.where(sub == s, row_b * root, out[v])
        out[v] = jnp.where(
            sub == s + 1, (top * next_b - side * row_b) * (root * lax.rsqrt(det)), out[v]
        )
        one, two = list(one), list(two)
        one[v] = one[v] - jnp.where(sub == s, 1.0, 0.0)
        two[v] = two[v] - jnp.where(sub == s + 1, 1.0, 0.0)
        first_coef = [(x * end - y * side) * inverse for x, y in zip(one, two)]
        next_coef = [(y * top - x * side) * inverse for x, y in zip(one, two)]
        for t in range(tiles):
            ra[t] = ra[t] - first_coef[t] * row_a - next_coef[t] * next_a
            rb[t] = rb[t] - first_coef[t] * row_b - next_coef[t] * next_b
        for m in range(j + 2, BLOCK):
            entry, following = rows_of(cols[m][v], s), rows_of(cols[m][v], s + 1)
            for t in range(tiles):
                change = first_coef[t] * entry + next_coef[t] * following
                cols[m][t] = cols[m][t] - change
    if first + tiles < len(a):
        for values, rows in ((a, ra), (b, rb)):
            for j in range(BLOCK):
                row = rows_of(rows[j // 8], j % 8)
                for u in range(tiles):
                    at = first + tiles + u
                    values[at] = values[at] - below[j][u] * row
    if later < len(a):
        solved = jnp.concatenate([jnp.concatenate(ra, 0), jnp.concatenate(rb, 0)], 1)

        def placed(value):
            parts = [value.astype(BF16)]
            if base:
                parts.insert(0, jnp.zeros((base, value.shape[1]), BF16))
            parts.append(jnp.zeros((8 * len(a) - base - BLOCK, value.shape[1]), BF16))
            return jnp.concatenate(parts, 0)

        w_high, w_middle, w_low = [placed(part) for part in split3(solved)]
        change = (
            jnp.dot(left, jnp.concatenate([w_high, w_high], 0), preferred_element_type=F32)
            + jnp.dot(left, jnp.concatenate([w_middle, w_middle], 0), preferred_element_type=F32)
            + jnp.dot(
                jnp.concatenate([l_high, l_low], 1),
                jnp.concatenate([w_low, w_high], 0),
                preferred_element_type=F32,
            )
        )
        for t in range(later, len(a)):
            rows = slice(8 * (t - later), 8 * (t - later) + 8)
            a[t] = a[t] - change[rows, :128]
            b[t] = b[t] - change[rows, 128:]
    return jnp.concatenate(out, 0)


NT = (((1,), (1,)), ((), ()))


class Gathered:
    def __init__(self, masks, count, members, side_ref, own_ref, *mate_refs):
        self.masks, self.count = masks, count
        self.me = lax.axis_index("blk") * members + lax.axis_index("grp")
        self.kind = parity(self.me, count)
        self.rows = own_ref.shape[1]
        self.dims = side_ref.shape[0] - 2
        self.vectors = own_ref.shape[0] - self.dims
        self.scale = side_ref[: self.dims, :]
        self.noise = side_ref[self.dims : self.dims + 1, :]
        self.pivots = side_ref[self.dims + 1 : self.dims + 2, :].astype(jnp.int32)
        self.points = lax.broadcasted_iota(jnp.int32, (self.rows, self.pivots.shape[1]), 0)
        self.own = own_ref[: self.dims, :] * self.scale
        lefts = [left_stack(self.own)]
        lefts += [left_stack(ref[: self.dims, :] * self.scale) for ref in mate_refs]
        self.left_own = jnp.concatenate([left.T.astype(BF16) for left in lefts], 0)

    def start(self):
        wide = jnp.zeros((self.left_own.shape[0], 2 * self.vectors), F32)
        narrow = jnp.zeros((self.left_own.shape[0], self.vectors), F32)
        return wide, narrow, jnp.zeros((3 * self.dims, self.pivots.shape[1]), F32)

    def owner(self, index, other):
        device, kind = self.me ^ other, self.kind ^ other
        for bit, (even, odd) in enumerate(zip(self.masks[0][:-1], self.masks[1][:-1])):
            device = device ^ (((index >> bit) & 1) * jnp.where(kind == 0, even, odd))
        return device

    def pick(self, total, ref, index, place, other):
        hots, parts = [], []
        for i in range(PICK):
            device = self.owner(place + index + i, other)
            hots.append((self.points == self.pivots - device * self.rows).astype(F32).astype(BF16))
            parts.append(jnp.concatenate(split3(ref[index + i, : self.dims, :]), 0).astype(BF16))
        return total + jnp.dot(
            jnp.concatenate(parts, 1), jnp.concatenate(hots, 0), preferred_element_type=F32
        )

    def add(self, wide, narrow, ref, index):
        blocks = [ref[index + i] for i in range(CHUNK)]
        right = jnp.concatenate(
            [right_stack(block[: self.dims] * self.scale) for block in blocks], 1
        )
        probe = jnp.concatenate([block[self.dims :] for block in blocks], 1)
        probe_high = probe.astype(BF16)
        probe_low = (probe - probe_high.astype(F32)).astype(BF16)
        value = matern(jnp.dot(self.left_own, right, preferred_element_type=F32))
        value_high = value.astype(BF16)
        value_low = (value - value_high.astype(F32)).astype(BF16)
        both = jnp.concatenate([probe_high, probe_low], 0)
        wide = wide + lax.dot_general(value_high, both, NT, preferred_element_type=F32)
        narrow = narrow + lax.dot_general(value_low, probe_high, NT, preferred_element_type=F32)
        return wide, narrow


def over(blocks, width, carry, visit):
    steps = blocks // width
    if blocks <= UNROLL:
        for i in range(steps):
            carry = visit(carry, i * width)
        return carry
    return lax.fori_loop(0, steps, lambda i, c: visit(c, i * width), carry)


def gathered_sum(wide, narrow):
    vectors = narrow.shape[1]
    return (wide[:, :vectors] + wide[:, vectors:] + narrow).T


def early_body(layout, side_ref, own_ref, mate_ref, part_ref, wide_ref, narrow_ref, picked_ref, parcel_ref):
    work = Gathered(*layout, side_ref, own_ref, mate_ref)
    wide, narrow, picked = work.start()
    blocks, rows = part_ref.shape[0], work.rows
    picked = over(blocks, PICK, picked, lambda c, i: work.pick(c, part_ref, i, 0, 0))
    wide, narrow = over(blocks, CHUNK, (wide, narrow), lambda c, i: work.add(*c, part_ref, i))
    wide_ref[...], narrow_ref[...], picked_ref[...] = wide[:rows], narrow[:rows], picked
    parcel_ref[0, : work.vectors, :] = gathered_sum(wide[rows:], narrow[rows:])
    parcel_ref[0, work.vectors :, :] = jnp.zeros((work.dims, rows), F32)
    parcel_ref[1] = picked


def middle_body(
    layout, place, side_ref, own_ref, part_ref, wide_in, narrow_in, picked_in,
    wide_ref, narrow_ref, picked_ref,
):
    work = Gathered(*layout, side_ref, own_ref)
    blocks = part_ref.shape[0]
    picked_ref[...] = over(
        blocks, PICK, picked_in[...], lambda c, i: work.pick(c, part_ref, i, place, 0)
    )
    wide_ref[...], narrow_ref[...] = over(
        blocks, CHUNK, (wide_in[...], narrow_in[...]), lambda c, i: work.add(*c, part_ref, i)
    )


def last_body(
    layout, side_ref, own_ref, there_ref, wide_ref, narrow_ref, picked_ref,
    panel_ref, product_ref, rows_ref, total_ref, sems, total_sem,
):
    work = Gathered(*layout, side_ref, own_ref)
    blocks = there_ref.shape[0] - 2
    picked = over(
        blocks,
        PICK,
        picked_ref[...] + there_ref[blocks + 1],
        lambda c, i: work.pick(c, there_ref, i, blocks, 1),
    )
    dims = work.dims
    pivot_x = (picked[:dims] + picked[dims : 2 * dims] + picked[2 * dims :]) * work.scale
    size = pivot_x.shape[1]
    left_pivot = left_stack(pivot_x).T.astype(BF16)
    both = jnp.concatenate([right_stack(pivot_x), right_stack(work.own)], 1)
    values = matern(jnp.dot(left_pivot, both, preferred_element_type=F32))
    eye = lax.broadcasted_iota(jnp.int32, (size, size), 0) == lax.broadcasted_iota(
        jnp.int32, (size, size), 1
    )
    inner = values[:, :size] + jnp.where(eye, work.noise, 0.0)
    a = [inner[i : i + 8] for i in range(0, size, 8)]
    b = [values[i : i + 8, size:] for i in range(0, size, 8)]

    wide, narrow = wide_ref[...], narrow_ref[...]
    wide, narrow = over(blocks, CHUNK, (wide, narrow), lambda c, i: work.add(*c, there_ref, i))
    total = gathered_sum(wide, narrow) + there_ref[blocks, : work.vectors, :]
    total_ref[...] = total + work.noise * own_ref[dims:, :]
    steps = size // BLOCK
    copies = []
    for step in range(steps):
        rows = pl.ds(step * BLOCK, BLOCK)
        rows_ref[rows, :] = eliminate(a, b, step)
        copies.append(
            pltpu.make_async_copy(rows_ref.at[rows, :], panel_ref.at[rows, :], sems.at[step])
        )
        copies[-1].start()
        if step == steps - 2:
            copies.append(pltpu.make_async_copy(total_ref, product_ref, total_sem))
            copies[-1].start()
    for copy in copies:
        copy.wait()


VMEM = pl.BlockSpec(memory_space=pltpu.VMEM)
PARAMS = pltpu.CompilerParams(vmem_limit_bytes=32 * 1024 * 1024)


def cost(points, rows):
    return pl.CostEstimate(
        flops=points * rows * 60, bytes_accessed=points * 100, transcendentals=points * rows * 2
    )


def sums(side, own):
    rows, vectors = own.shape[1], own.shape[0] - side.shape[0] + 2
    return (
        jax.ShapeDtypeStruct((rows, 2 * vectors), F32),
        jax.ShapeDtypeStruct((rows, vectors), F32),
        jax.ShapeDtypeStruct((3 * (side.shape[0] - 2), side.shape[1]), F32),
    )


def early(layout, side, own, mate, part):
    rows = own.shape[1]
    return pl.pallas_call(
        functools.partial(early_body, layout),
        out_shape=sums(side, own) + (jax.ShapeDtypeStruct((2,) + own.shape, F32),),
        in_specs=[VMEM] * 4,
        out_specs=(VMEM,) * 4,
        cost_estimate=cost(part.shape[0] * rows, 2 * rows),
        compiler_params=PARAMS,
    )(side, own, mate, part)


def middle(layout, place, side, own, part, *carry):
    rows = own.shape[1]
    return pl.pallas_call(
        functools.partial(middle_body, layout, place),
        out_shape=sums(side, own),
        in_specs=[VMEM] * 6,
        out_specs=(VMEM,) * 3,
        cost_estimate=cost(part.shape[0] * rows, rows),
        compiler_params=PARAMS,
    )(side, own, part, *carry)


def finish(layout, side, own, there, *carry):
    size, rows = side.shape[1], own.shape[1]
    product = (own.shape[0] - side.shape[0] + 2, rows)
    return pl.pallas_call(
        functools.partial(last_body, layout),
        out_shape=(
            jax.ShapeDtypeStruct((size, rows), F32),
            jax.ShapeDtypeStruct(product, F32),
        ),
        in_specs=[VMEM] * (3 + len(carry)),
        out_specs=(pl.BlockSpec(memory_space=pl.ANY),) * 2,
        scratch_shapes=[
            pltpu.VMEM((size, rows), F32),
            pltpu.VMEM(product, F32),
            pltpu.SemaphoreType.DMA((size // BLOCK,)),
            pltpu.SemaphoreType.DMA,
        ],
        compiler_params=PARAMS,
    )(side, own, there, *carry)


def solution(mesh):
    groups, members = mesh.shape["blk"], mesh.shape["grp"]
    count = groups * members
    masks = exchange_masks(groups, members)

    def swap(value, step):
        pairs = [(i, i ^ masks[parity(i, count)][step]) for i in range(count)]
        return lax.ppermute(value, ("blk", "grp"), pairs)

    def local(inputs, probes, lengths, noise, pivots):
        rows = inputs.shape[1]
        own = jnp.concatenate([inputs, probes], 0)
        layout = (masks, count, members)
        last = len(masks[0]) - 1
        here = own[None]
        for step in range(last - 1):
            if step == 1:
                side = jnp.concatenate(
                    [
                        jnp.broadcast_to((SCALE / lengths)[:, None], inputs.shape),
                        jnp.broadcast_to(noise[:, None], (1, rows)),
                        pivots.astype(F32)[None, :],
                    ],
                    0,
                )
            if step == 1:
                mate = swap(lax.optimization_barrier((own, here))[0], last)
            here = jnp.concatenate([here, swap(here, step)], 0)
        arrived = swap(here, last - 1)
        *carry, parcel = early(layout, side, own, mate, here)
        arrived, parcel = lax.optimization_barrier((arrived, parcel))
        there = swap(jnp.concatenate([arrived, parcel], 0), last)
        carry = middle(layout, here.shape[0], side, own, arrived, *carry)
        return finish(layout, side, own, there, *carry)

    in_specs = (P(None, ("blk", "grp")), P(None, ("blk", "grp")), P(), P(), P())
    out_specs = (P(None, ("blk", "grp")), P(None, ("blk", "grp")))
    return jax.shard_map(local, mesh=mesh, in_specs=in_specs, out_specs=out_specs, check_vma=False)
```

```python
import functools
import math

import jax
import jax.numpy as jnp
from jax import lax
from jax.experimental import pallas as pl
from jax.experimental.pallas import tpu as pltpu
from jax.sharding import PartitionSpec as P

F32 = jnp.float32
BF16 = jnp.bfloat16
LN2 = math.log(2.0)
SCALE = math.sqrt(5.0) / LN2
BLOCK = 16
CHUNK = 8
PICK = 4
UNROLL = 32


def exchange_masks(groups, members):
    low = members.bit_length() - 1
    bits = [1 << bit for bit in range(low - 1, 1, -1)]
    bits += [1 << (low + bit) for bit in range(groups.bit_length() - 2, -1, -1)]
    bits += [2] if members > 2 else []
    even = [bit | 1 for bit in bits]
    odd = even[:-2] + even[:-3:-1]
    return even + [1], odd + [1]


def parity(index, count):
    bits = 0
    for bit in range(count.bit_length() - 1):
        bits = bits ^ (index >> bit)
    return bits & 1


def split3(value):
    high = value.astype(BF16).astype(F32)
    rest = value - high
    middle = rest.astype(BF16).astype(F32)
    return high, middle, rest - middle


def norm_tile(x, first):
    high, middle, low = split3(jnp.sum(x * x, axis=0, keepdims=True))
    row = lax.broadcasted_iota(jnp.int32, x.shape, 0)
    if not first:
        row = jnp.where(row < 3, row + 3, row - 3)
    tile = jnp.where(row < 6, 1.0, 0.0)
    tile = jnp.where(row == 0, high, tile)
    tile = jnp.where(row == 1, middle, tile)
    return jnp.where(row == 2, low, tile)


def left_stack(x):
    high, middle, low = split3(x)
    return jnp.concatenate(
        [high, high, high, middle, middle, low, norm_tile(x, True), jnp.zeros_like(x)], 0
    )


def right_stack(x):
    high, middle, low = split3(-2.0 * x)
    return jnp.concatenate(
        [high, middle, low, high, middle, high, norm_tile(x, False), jnp.zeros_like(x)], 0
    ).astype(BF16)


def matern(square):
    square = jnp.maximum(square, 1e-30)
    radius = square * lax.rsqrt(square)
    return (1.0 + LN2 * radius + (LN2 * LN2 / 3.0) * square) * jnp.exp2(-radius)


def rows_of(value, row):
    return jnp.broadcast_to(value[row : row + 1, :], value.shape)


def eliminate(a, b, step):
    tiles = BLOCK // 8
    base, first = step * BLOCK, step * tiles
    later = first + 2 * tiles
    sub = lax.broadcasted_iota(jnp.int32, (8, 128), 0)

    def column(piece, m):
        return jnp.broadcast_to(piece[:, base + m : base + m + 1], (8, 128))

    ra, rb = a[first : first + tiles], b[first : first + tiles]
    cols = [[column(piece, m) for piece in ra] for m in range(BLOCK)]
    below = [[column(piece, m) for piece in a[first + tiles : later]] for m in range(BLOCK)]
    if later < len(a):
        l_high, l_middle, l_low = [
            part.astype(BF16) for part in split3(jnp.concatenate(a[later:], 0))
        ]
        left = jnp.concatenate([l_high, l_middle], 1)
    out = [jnp.zeros((8, 128), F32) for t in range(tiles)]
    for j in range(0, BLOCK, 2):
        v, s = divmod(j, 8)
        one, two = cols[j], cols[j + 1]
        top, side, end = rows_of(one[v], s), rows_of(one[v], s + 1), rows_of(two[v], s + 1)
        det = top * end - side * side
        inverse = 1.0 / det
        row_a, next_a = rows_of(ra[v], s), rows_of(ra[v], s + 1)
        row_b, next_b = rows_of(rb[v], s), rows_of(rb[v], s + 1)
        root = lax.rsqrt(top)
        out[v] = jnp.where(sub == s, row_b * root, out[v])
        out[v] = jnp.where(
            sub == s + 1, (top * next_b - side * row_b) * (root * lax.rsqrt(det)), out[v]
        )
        one, two = list(one), list(two)
        one[v] = one[v] - jnp.where(sub == s, 1.0, 0.0)
        two[v] = two[v] - jnp.where(sub == s + 1, 1.0, 0.0)
        first_coef = [(x * end - y * side) * inverse for x, y in zip(one, two)]
        next_coef = [(y * top - x * side) * inverse for x, y in zip(one, two)]
        for t in range(tiles):
            ra[t] = ra[t] - first_coef[t] * row_a - next_coef[t] * next_a
            rb[t] = rb[t] - first_coef[t] * row_b - next_coef[t] * next_b
        for m in range(j + 2, BLOCK):
            entry, following = rows_of(cols[m][v], s), rows_of(cols[m][v], s + 1)
            for t in range(tiles):
                change = first_coef[t] * entry + next_coef[t] * following
                cols[m][t] = cols[m][t] - change
    if first + tiles < len(a):
        for values, rows in ((a, ra), (b, rb)):
            for j in range(BLOCK):
                row = rows_of(rows[j // 8], j % 8)
                for u in range(tiles):
                    at = first + tiles + u
                    values[at] = values[at] - below[j][u] * row
    if later < len(a):
        solved = jnp.concatenate([jnp.concatenate(ra, 0), jnp.concatenate(rb, 0)], 1)

        def placed(value):
            parts = [value.astype(BF16)]
            if base:
                parts.insert(0, jnp.zeros((base, value.shape[1]), BF16))
            parts.append(jnp.zeros((8 * len(a) - base - BLOCK, value.shape[1]), BF16))
            return jnp.concatenate(parts, 0)

        w_high, w_middle, w_low = [placed(part) for part in split3(solved)]
        change = (
            jnp.dot(left, jnp.concatenate([w_high, w_high], 0), preferred_element_type=F32)
            + jnp.dot(left, jnp.concatenate([w_middle, w_middle], 0), preferred_element_type=F32)
            + jnp.dot(
                jnp.concatenate([l_high, l_low], 1),
                jnp.concatenate([w_low, w_high], 0),
                preferred_element_type=F32,
            )
        )
        for t in range(later, len(a)):
            rows = slice(8 * (t - later), 8 * (t - later) + 8)
            a[t] = a[t] - change[rows, :128]
            b[t] = b[t] - change[rows, 128:]
    return jnp.concatenate(out, 0)


NT = (((1,), (1,)), ((), ()))


class Gathered:
    def __init__(self, masks, count, members, side_ref, own_ref, *mate_refs):
        self.masks, self.count = masks, count
        self.me = lax.axis_index("blk") * members + lax.axis_index("grp")
        self.kind = parity(self.me, count)
        self.rows = own_ref.shape[1]
        self.dims = side_ref.shape[0] - 2
        self.vectors = own_ref.shape[0] - self.dims
        self.scale = side_ref[: self.dims, :]
        self.noise = side_ref[self.dims : self.dims + 1, :]
        self.pivots = side_ref[self.dims + 1 : self.dims + 2, :].astype(jnp.int32)
        self.points = lax.broadcasted_iota(jnp.int32, (self.rows, self.pivots.shape[1]), 0)
        self.own = own_ref[: self.dims, :] * self.scale
        lefts = [left_stack(self.own)]
        lefts += [left_stack(ref[: self.dims, :] * self.scale) for ref in mate_refs]
        self.left_own = jnp.concatenate([left.T.astype(BF16) for left in lefts], 0)

    def start(self):
        wide = jnp.zeros((self.left_own.shape[0], 2 * self.vectors), F32)
        narrow = jnp.zeros((self.left_own.shape[0], self.vectors), F32)
        return wide, narrow, jnp.zeros((3 * self.dims, self.pivots.shape[1]), F32)

    def owner(self, index, other):
        device, kind = self.me ^ other, self.kind ^ other
        for bit, (even, odd) in enumerate(zip(self.masks[0][:-1], self.masks[1][:-1])):
            device = device ^ (((index >> bit) & 1) * jnp.where(kind == 0, even, odd))
        return device

    def pick(self, total, ref, index, place, other):
        hots, parts = [], []
        for i in range(PICK):
            device = self.owner(place + index + i, other)
            hots.append((self.points == self.pivots - device * self.rows).astype(F32).astype(BF16))
            parts.append(jnp.concatenate(split3(ref[index + i, : self.dims, :]), 0).astype(BF16))
        return total + jnp.dot(
            jnp.concatenate(parts, 1), jnp.concatenate(hots, 0), preferred_element_type=F32
        )

    def add(self, wide, narrow, ref, index):
        blocks = [ref[index + i] for i in range(CHUNK)]
        right = jnp.concatenate(
            [right_stack(block[: self.dims] * self.scale) for block in blocks], 1
        )
        probe = jnp.concatenate([block[self.dims :] for block in blocks], 1)
        probe_high = probe.astype(BF16)
        probe_low = (probe - probe_high.astype(F32)).astype(BF16)
        value = matern(jnp.dot(self.left_own, right, preferred_element_type=F32))
        value_high = value.astype(BF16)
        value_low = (value - value_high.astype(F32)).astype(BF16)
        both = jnp.concatenate([probe_high, probe_low], 0)
        wide = wide + lax.dot_general(value_high, both, NT, preferred_element_type=F32)
        narrow = narrow + lax.dot_general(value_low, probe_high, NT, preferred_element_type=F32)
        return wide, narrow


def over(blocks, width, carry, visit):
    steps = blocks // width
    if blocks <= UNROLL:
        for i in range(steps):
            carry = visit(carry, i * width)
        return carry
    return lax.fori_loop(0, steps, lambda i, c: visit(c, i * width), carry)


def gathered_sum(wide, narrow):
    vectors = narrow.shape[1]
    return (wide[:, :vectors] + wide[:, vectors:] + narrow).T


def picked_sum(picked, dims):
    return picked[:dims] + picked[dims : 2 * dims] + picked[2 * dims :]


def early_body(layout, side_ref, own_ref, mate_ref, part_ref, share_ref, parcel_ref):
    work = Gathered(*layout, side_ref, own_ref, mate_ref)
    wide, narrow, picked = work.start()
    blocks, rows, vectors = part_ref.shape[0], work.rows, work.vectors
    picked = over(blocks, PICK, picked, lambda c, i: work.pick(c, part_ref, i, 0, 0))
    wide, narrow = over(blocks, CHUNK, (wide, narrow), lambda c, i: work.add(*c, part_ref, i))
    found = picked_sum(picked, work.dims)
    share_ref[:vectors, :] = gathered_sum(wide[:rows], narrow[:rows])
    share_ref[vectors:, :] = found
    parcel_ref[0, :vectors, :] = gathered_sum(wide[rows:], narrow[rows:])
    parcel_ref[0, vectors:, :] = found


def middle_body(layout, place, side_ref, own_ref, part_ref, share_ref, out_ref):
    work = Gathered(*layout, side_ref, own_ref)
    wide, narrow, picked = work.start()
    blocks, vectors = part_ref.shape[0], work.vectors
    picked = over(blocks, PICK, picked, lambda c, i: work.pick(c, part_ref, i, place, 0))
    wide, narrow = over(blocks, CHUNK, (wide, narrow), lambda c, i: work.add(*c, part_ref, i))
    out_ref[:vectors, :] = share_ref[:vectors, :] + gathered_sum(wide, narrow)
    out_ref[vectors:, :] = share_ref[vectors:, :] + picked_sum(picked, work.dims)


def last_body(
    layout, side_ref, own_ref, there_ref, share_ref,
    panel_ref, product_ref, rows_ref, total_ref, sems, total_sem,
):
    work = Gathered(*layout, side_ref, own_ref)
    blocks, dims, vectors = there_ref.shape[0] - 1, work.dims, work.vectors
    wide, narrow, picked = work.start()
    picked = over(blocks, PICK, picked, lambda c, i: work.pick(c, there_ref, i, blocks, 1))
    found = share_ref[vectors:, :] + there_ref[blocks, vectors:, :]
    pivot_x = (found + picked_sum(picked, dims)) * work.scale
    size = pivot_x.shape[1]
    left_pivot = left_stack(pivot_x).T.astype(BF16)
    both = jnp.concatenate([right_stack(pivot_x), right_stack(work.own)], 1)
    values = matern(jnp.dot(left_pivot, both, preferred_element_type=F32))
    eye = lax.broadcasted_iota(jnp.int32, (size, size), 0) == lax.broadcasted_iota(
        jnp.int32, (size, size), 1
    )
    inner = values[:, :size] + jnp.where(eye, work.noise, 0.0)
    a = [inner[i : i + 8] for i in range(0, size, 8)]
    b = [values[i : i + 8, size:] for i in range(0, size, 8)]

    wide, narrow = over(blocks, CHUNK, (wide, narrow), lambda c, i: work.add(*c, there_ref, i))
    total = gathered_sum(wide, narrow) + there_ref[blocks, :vectors, :] + share_ref[:vectors, :]
    total_ref[...] = total + work.noise * own_ref[dims:, :]
    steps = size // BLOCK
    copies = []
    for step in range(steps):
        rows = pl.ds(step * BLOCK, BLOCK)
        rows_ref[rows, :] = eliminate(a, b, step)
        copies.append(
            pltpu.make_async_copy(rows_ref.at[rows, :], panel_ref.at[rows, :], sems.at[step])
        )
        copies[-1].start()
        if step == steps // 2:
            copies.append(pltpu.make_async_copy(total_ref, product_ref, total_sem))
            copies[-1].start()
    for copy in copies:
        copy.wait()


VMEM = pl.BlockSpec(memory_space=pltpu.VMEM)
PARAMS = pltpu.CompilerParams(vmem_limit_bytes=32 * 1024 * 1024)


def cost(points, rows):
    return pl.CostEstimate(
        flops=points * rows * 60, bytes_accessed=points * 100, transcendentals=points * rows * 2
    )


def early(layout, side, own, mate, part):
    rows = own.shape[1]
    return pl.pallas_call(
        functools.partial(early_body, layout),
        out_shape=(
            jax.ShapeDtypeStruct(own.shape, F32),
            jax.ShapeDtypeStruct((1,) + own.shape, F32),
        ),
        in_specs=[VMEM] * 4,
        out_specs=(VMEM,) * 2,
        cost_estimate=cost(part.shape[0] * rows, 2 * rows),
        compiler_params=PARAMS,
    )(side, own, mate, part)


def middle(layout, place, side, own, part, share):
    rows = own.shape[1]
    return pl.pallas_call(
        functools.partial(middle_body, layout, place),
        out_shape=jax.ShapeDtypeStruct(own.shape, F32),
        in_specs=[VMEM] * 4,
        out_specs=VMEM,
        cost_estimate=cost(part.shape[0] * rows, rows),
        compiler_params=PARAMS,
    )(side, own, part, share)


def finish(layout, side, own, there, *carry):
    size, rows = side.shape[1], own.shape[1]
    product = (own.shape[0] - side.shape[0] + 2, rows)
    return pl.pallas_call(
        functools.partial(last_body, layout),
        out_shape=(
            jax.ShapeDtypeStruct((size, rows), F32),
            jax.ShapeDtypeStruct(product, F32),
        ),
        in_specs=[VMEM] * (3 + len(carry)),
        out_specs=(pl.BlockSpec(memory_space=pl.ANY),) * 2,
        scratch_shapes=[
            pltpu.VMEM((size, rows), F32),
            pltpu.VMEM(product, F32),
            pltpu.SemaphoreType.DMA((size // BLOCK,)),
            pltpu.SemaphoreType.DMA,
        ],
        compiler_params=PARAMS,
    )(side, own, there, *carry)


def solution(mesh):
    groups, members = mesh.shape["blk"], mesh.shape["grp"]
    count = groups * members
    masks = exchange_masks(groups, members)

    def swap(value, step):
        pairs = [(i, i ^ masks[parity(i, count)][step]) for i in range(count)]
        return lax.ppermute(value, ("blk", "grp"), pairs)

    def local(inputs, probes, lengths, noise, pivots):
        rows = inputs.shape[1]
        own = jnp.concatenate([inputs, probes], 0)
        layout = (masks, count, members)
        last = len(masks[0]) - 1
        here = own[None]
        for step in range(last - 1):
            if step == 1:
                side = jnp.concatenate(
                    [
                        jnp.broadcast_to((SCALE / lengths)[:, None], inputs.shape),
                        jnp.broadcast_to(noise[:, None], (1, rows)),
                        pivots.astype(F32)[None, :],
                    ],
                    0,
                )
            if step == 1:
                mate = swap(lax.optimization_barrier((own, here))[0], last)
            here = jnp.concatenate([here, swap(here, step)], 0)
        arrived = swap(here, last - 1)
        share, parcel = early(layout, side, own, mate, here)
        arrived, parcel = lax.optimization_barrier((arrived, parcel))
        there = swap(jnp.concatenate([arrived, parcel], 0), last)
        share = middle(layout, here.shape[0], side, own, arrived, share)
        return finish(layout, side, own, there, share)

    in_specs = (P(None, ("blk", "grp")), P(None, ("blk", "grp")), P(), P(), P())
    out_specs = (P(None, ("blk", "grp")), P(None, ("blk", "grp")))
    return jax.shard_map(local, mesh=mesh, in_specs=in_specs, out_specs=out_specs, check_vma=False)
```

```python
import functools
import math

import jax
import jax.numpy as jnp
from jax import lax
from jax.experimental import pallas as pl
from jax.experimental.pallas import tpu as pltpu
from jax.sharding import PartitionSpec as P

F32 = jnp.float32
BF16 = jnp.bfloat16
LN2 = math.log(2.0)
SCALE = math.sqrt(5.0) / LN2
BLOCK = 16
CHUNK = 8
PICK = 4
UNROLL = 32


def exchange_masks(groups, members):
    low = members.bit_length() - 1
    bits = [1 << bit for bit in range(low - 1, 1, -1)]
    bits += [1 << (low + bit) for bit in range(groups.bit_length() - 2, -1, -1)]
    bits += [2] if members > 2 else []
    even = [bit | 1 for bit in bits]
    odd = even[:-2] + even[:-3:-1]
    return even + [1], odd + [1]


def parity(index, count):
    bits = 0
    for bit in range(count.bit_length() - 1):
        bits = bits ^ (index >> bit)
    return bits & 1


def split3(value):
    high = value.astype(BF16).astype(F32)
    rest = value - high
    middle = rest.astype(BF16).astype(F32)
    return high, middle, rest - middle


def norm_tile(x, first):
    high, middle, low = split3(jnp.sum(x * x, axis=0, keepdims=True))
    row = lax.broadcasted_iota(jnp.int32, x.shape, 0)
    if not first:
        row = jnp.where(row < 3, row + 3, row - 3)
    tile = jnp.where(row < 6, 1.0, 0.0)
    tile = jnp.where(row == 0, high, tile)
    tile = jnp.where(row == 1, middle, tile)
    return jnp.where(row == 2, low, tile)


def left_stack(x):
    high, middle, low = split3(x)
    return jnp.concatenate(
        [high, high, high, middle, middle, low, norm_tile(x, True), jnp.zeros_like(x)], 0
    )


def right_stack(x):
    high, middle, low = split3(-2.0 * x)
    return jnp.concatenate(
        [high, middle, low, high, middle, high, norm_tile(x, False), jnp.zeros_like(x)], 0
    ).astype(BF16)


def matern(square):
    square = jnp.maximum(square, 1e-30)
    radius = square * lax.rsqrt(square)
    return (1.0 + LN2 * radius + (LN2 * LN2 / 3.0) * square) * jnp.exp2(-radius)


def rows_of(value, row):
    return jnp.broadcast_to(value[row : row + 1, :], value.shape)


def eliminate(a, b, step):
    tiles = BLOCK // 8
    base, first = step * BLOCK, step * tiles
    later = first + 2 * tiles
    sub = lax.broadcasted_iota(jnp.int32, (8, 128), 0)

    def column(piece, m):
        return jnp.broadcast_to(piece[:, base + m : base + m + 1], (8, 128))

    ra, rb = a[first : first + tiles], b[first : first + tiles]
    cols = [[column(piece, m) for piece in ra] for m in range(BLOCK)]
    below = [[column(piece, m) for piece in a[first + tiles : later]] for m in range(BLOCK)]
    if later < len(a):
        l_high, l_middle, l_low = [
            part.astype(BF16) for part in split3(jnp.concatenate(a[later:], 0))
        ]
        left = jnp.concatenate([l_high, l_middle], 1)
    out = [jnp.zeros((8, 128), F32) for t in range(tiles)]
    for j in range(0, BLOCK, 2):
        v, s = divmod(j, 8)
        one, two = cols[j], cols[j + 1]
        top, side, end = rows_of(one[v], s), rows_of(one[v], s + 1), rows_of(two[v], s + 1)
        det = top * end - side * side
        inverse = 1.0 / det
        row_a, next_a = rows_of(ra[v], s), rows_of(ra[v], s + 1)
        row_b, next_b = rows_of(rb[v], s), rows_of(rb[v], s + 1)
        root = lax.rsqrt(top)
        out[v] = jnp.where(sub == s, row_b * root, out[v])
        out[v] = jnp.where(
            sub == s + 1, (top * next_b - side * row_b) * (root * lax.rsqrt(det)), out[v]
        )
        one, two = list(one), list(two)
        one[v] = one[v] - jnp.where(sub == s, 1.0, 0.0)
        two[v] = two[v] - jnp.where(sub == s + 1, 1.0, 0.0)
        first_coef = [(x * end - y * side) * inverse for x, y in zip(one, two)]
        next_coef = [(y * top - x * side) * inverse for x, y in zip(one, two)]
        for t in range(tiles):
            ra[t] = ra[t] - first_coef[t] * row_a - next_coef[t] * next_a
            rb[t] = rb[t] - first_coef[t] * row_b - next_coef[t] * next_b
        for m in range(j + 2, BLOCK):
            entry, following = rows_of(cols[m][v], s), rows_of(cols[m][v], s + 1)
            for t in range(tiles):
                change = first_coef[t] * entry + next_coef[t] * following
                cols[m][t] = cols[m][t] - change
    if first + tiles < len(a):
        for values, rows in ((a, ra), (b, rb)):
            for j in range(BLOCK):
                row = rows_of(rows[j // 8], j % 8)
                for u in range(tiles):
                    at = first + tiles + u
                    values[at] = values[at] - below[j][u] * row
    if later < len(a):
        solved = jnp.concatenate([jnp.concatenate(ra, 0), jnp.concatenate(rb, 0)], 1)

        def placed(value):
            parts = [value.astype(BF16)]
            if base:
                parts.insert(0, jnp.zeros((base, value.shape[1]), BF16))
            parts.append(jnp.zeros((8 * len(a) - base - BLOCK, value.shape[1]), BF16))
            return jnp.concatenate(parts, 0)

        w_high, w_middle, w_low = [placed(part) for part in split3(solved)]
        change = (
            jnp.dot(left, jnp.concatenate([w_high, w_high], 0), preferred_element_type=F32)
            + jnp.dot(left, jnp.concatenate([w_middle, w_middle], 0), preferred_element_type=F32)
            + jnp.dot(
                jnp.concatenate([l_high, l_low], 1),
                jnp.concatenate([w_low, w_high], 0),
                preferred_element_type=F32,
            )
        )
        for t in range(later, len(a)):
            rows = slice(8 * (t - later), 8 * (t - later) + 8)
            a[t] = a[t] - change[rows, :128]
            b[t] = b[t] - change[rows, 128:]
    return jnp.concatenate(out, 0)


NT = (((1,), (1,)), ((), ()))


class Gathered:
    def __init__(self, masks, count, members, side_ref, own_ref, *mate_refs):
        self.masks, self.count = masks, count
        self.me = lax.axis_index("blk") * members + lax.axis_index("grp")
        self.kind = parity(self.me, count)
        self.rows = own_ref.shape[1]
        self.dims = side_ref.shape[0] - 2
        self.vectors = own_ref.shape[0] - self.dims
        self.scale = side_ref[: self.dims, :]
        self.noise = side_ref[self.dims : self.dims + 1, :]
        self.pivots = side_ref[self.dims + 1 : self.dims + 2, :].astype(jnp.int32)
        self.points = lax.broadcasted_iota(jnp.int32, (self.rows, self.pivots.shape[1]), 0)
        self.own = own_ref[: self.dims, :] * self.scale
        lefts = [left_stack(self.own)]
        lefts += [left_stack(ref[: self.dims, :] * self.scale) for ref in mate_refs]
        self.left_own = jnp.concatenate([left.T.astype(BF16) for left in lefts], 0)

    def start(self):
        wide = jnp.zeros((self.left_own.shape[0], 2 * self.vectors), F32)
        narrow = jnp.zeros((self.left_own.shape[0], self.vectors), F32)
        return wide, narrow, jnp.zeros((3 * self.dims, self.pivots.shape[1]), F32)

    def owner(self, index, other):
        device, kind = self.me ^ other, self.kind ^ other
        for bit, (even, odd) in enumerate(zip(self.masks[0][:-1], self.masks[1][:-1])):
            device = device ^ (((index >> bit) & 1) * jnp.where(kind == 0, even, odd))
        return device

    def pick(self, total, ref, index, place, other):
        hots, parts = [], []
        for i in range(PICK):
            device = self.owner(place + index + i, other)
            hots.append((self.points == self.pivots - device * self.rows).astype(F32).astype(BF16))
            parts.append(jnp.concatenate(split3(ref[index + i, : self.dims, :]), 0).astype(BF16))
        return total + jnp.dot(
            jnp.concatenate(parts, 1), jnp.concatenate(hots, 0), preferred_element_type=F32
        )

    def add(self, wide, narrow, ref, index):
        blocks = [ref[index + i] for i in range(CHUNK)]
        right = jnp.concatenate(
            [right_stack(block[: self.dims] * self.scale) for block in blocks], 1
        )
        probe = jnp.concatenate([block[self.dims :] for block in blocks], 1)
        probe_high = probe.astype(BF16)
        probe_low = (probe - probe_high.astype(F32)).astype(BF16)
        value = matern(jnp.dot(self.left_own, right, preferred_element_type=F32))
        value_high = value.astype(BF16)
        value_low = (value - value_high.astype(F32)).astype(BF16)
        both = jnp.concatenate([probe_high, probe_low], 0)
        wide = wide + lax.dot_general(value_high, both, NT, preferred_element_type=F32)
        narrow = narrow + lax.dot_general(value_low, probe_high, NT, preferred_element_type=F32)
        return wide, narrow


def over(blocks, width, carry, visit):
    steps = blocks // width
    if blocks <= UNROLL:
        for i in range(steps):
            carry = visit(carry, i * width)
        return carry
    return lax.fori_loop(0, steps, lambda i, c: visit(c, i * width), carry)


def gathered_sum(wide, narrow):
    vectors = narrow.shape[1]
    return (wide[:, :vectors] + wide[:, vectors:] + narrow).T


def picked_sum(picked, dims):
    return picked[:dims] + picked[dims : 2 * dims] + picked[2 * dims :]


def early_body(layout, side_ref, own_ref, mate_ref, part_ref, share_ref, parcel_ref):
    work = Gathered(*layout, side_ref, own_ref, mate_ref)
    wide, narrow, picked = work.start()
    blocks, rows, vectors = part_ref.shape[0], work.rows, work.vectors
    picked = over(blocks, PICK, picked, lambda c, i: work.pick(c, part_ref, i, 0, 0))
    wide, narrow = over(blocks, CHUNK, (wide, narrow), lambda c, i: work.add(*c, part_ref, i))
    found = picked_sum(picked, work.dims)
    share_ref[:vectors, :] = gathered_sum(wide[:rows], narrow[:rows])
    share_ref[vectors:, :] = found
    parcel_ref[0, :vectors, :] = gathered_sum(wide[rows:], narrow[rows:])
    parcel_ref[0, vectors:, :] = found


def middle_body(layout, place, side_ref, own_ref, part_ref, share_ref, out_ref):
    work = Gathered(*layout, side_ref, own_ref)
    wide, narrow, picked = work.start()
    blocks, vectors = part_ref.shape[0], work.vectors
    picked = over(blocks, PICK, picked, lambda c, i: work.pick(c, part_ref, i, place, 0))
    wide, narrow = over(blocks, CHUNK, (wide, narrow), lambda c, i: work.add(*c, part_ref, i))
    out_ref[:vectors, :] = share_ref[:vectors, :] + gathered_sum(wide, narrow)
    out_ref[vectors:, :] = share_ref[vectors:, :] + picked_sum(picked, work.dims)


def last_body(
    layout, side_ref, own_ref, there_ref, share_ref,
    panel_ref, product_ref, rows_ref, total_ref, sems, total_sem,
):
    work = Gathered(*layout, side_ref, own_ref)
    blocks, dims, vectors = there_ref.shape[0] - 1, work.dims, work.vectors
    wide, narrow, picked = work.start()
    picked = over(blocks, PICK, picked, lambda c, i: work.pick(c, there_ref, i, blocks, 1))
    found = share_ref[vectors:, :] + there_ref[blocks, vectors:, :]
    pivot_x = (found + picked_sum(picked, dims)) * work.scale
    size = pivot_x.shape[1]
    left_pivot = left_stack(pivot_x).T.astype(BF16)
    both = jnp.concatenate([right_stack(pivot_x), right_stack(work.own)], 1)
    values = matern(jnp.dot(left_pivot, both, preferred_element_type=F32))
    eye = lax.broadcasted_iota(jnp.int32, (size, size), 0) == lax.broadcasted_iota(
        jnp.int32, (size, size), 1
    )
    inner = values[:, :size] + jnp.where(eye, work.noise, 0.0)
    a = [inner[i : i + 8] for i in range(0, size, 8)]
    b = [values[i : i + 8, size:] for i in range(0, size, 8)]

    wide, narrow = over(blocks, CHUNK, (wide, narrow), lambda c, i: work.add(*c, there_ref, i))
    total = gathered_sum(wide, narrow) + there_ref[blocks, :vectors, :] + share_ref[:vectors, :]
    total_ref[...] = total + work.noise * own_ref[dims:, :]
    steps = size // BLOCK
    copies = []
    for step in range(steps):
        rows = pl.ds(step * BLOCK, BLOCK)
        rows_ref[rows, :] = eliminate(a, b, step)
        copies.append(
            pltpu.make_async_copy(rows_ref.at[rows, :], panel_ref.at[rows, :], sems.at[step])
        )
        copies[-1].start()
        if step == steps - 2:
            copies.append(pltpu.make_async_copy(total_ref, product_ref, total_sem))
            copies[-1].start()
    for copy in copies:
        copy.wait()


VMEM = pl.BlockSpec(memory_space=pltpu.VMEM)
PARAMS = pltpu.CompilerParams(vmem_limit_bytes=32 * 1024 * 1024)


def cost(points, rows):
    return pl.CostEstimate(
        flops=points * rows * 60, bytes_accessed=points * 100, transcendentals=points * rows * 2
    )


def early(layout, side, own, mate, part):
    rows = own.shape[1]
    return pl.pallas_call(
        functools.partial(early_body, layout),
        out_shape=(
            jax.ShapeDtypeStruct(own.shape, F32),
            jax.ShapeDtypeStruct((1,) + own.shape, F32),
        ),
        in_specs=[VMEM] * 4,
        out_specs=(VMEM,) * 2,
        cost_estimate=cost(part.shape[0] * rows, 2 * rows),
        compiler_params=PARAMS,
    )(side, own, mate, part)


def middle(layout, place, side, own, part, share):
    rows = own.shape[1]
    return pl.pallas_call(
        functools.partial(middle_body, layout, place),
        out_shape=jax.ShapeDtypeStruct(own.shape, F32),
        in_specs=[VMEM] * 4,
        out_specs=VMEM,
        cost_estimate=cost(part.shape[0] * rows, rows),
        compiler_params=PARAMS,
    )(side, own, part, share)


def finish(layout, side, own, there, *carry):
    size, rows = side.shape[1], own.shape[1]
    product = (own.shape[0] - side.shape[0] + 2, rows)
    return pl.pallas_call(
        functools.partial(last_body, layout),
        out_shape=(
            jax.ShapeDtypeStruct((size, rows), F32),
            jax.ShapeDtypeStruct(product, F32),
        ),
        in_specs=[VMEM] * (3 + len(carry)),
        out_specs=(pl.BlockSpec(memory_space=pl.ANY),) * 2,
        scratch_shapes=[
            pltpu.VMEM((size, rows), F32),
            pltpu.VMEM(product, F32),
            pltpu.SemaphoreType.DMA((size // BLOCK,)),
            pltpu.SemaphoreType.DMA,
        ],
        compiler_params=PARAMS,
    )(side, own, there, *carry)


def solution(mesh):
    groups, members = mesh.shape["blk"], mesh.shape["grp"]
    count = groups * members
    masks = exchange_masks(groups, members)

    def swap(value, step):
        pairs = [(i, i ^ masks[parity(i, count)][step]) for i in range(count)]
        return lax.ppermute(value, ("blk", "grp"), pairs)

    def local(inputs, probes, lengths, noise, pivots):
        rows = inputs.shape[1]
        own = jnp.concatenate([inputs, probes], 0)
        layout = (masks, count, members)
        last = len(masks[0]) - 1
        here = own[None]
        for step in range(last - 1):
            if step == 1:
                side = jnp.concatenate(
                    [
                        jnp.broadcast_to((SCALE / lengths)[:, None], inputs.shape),
                        jnp.broadcast_to(noise[:, None], (1, rows)),
                        pivots.astype(F32)[None, :],
                    ],
                    0,
                )
            if step == 1:
                mate = swap(lax.optimization_barrier((own, here))[0], last)
            here = jnp.concatenate([here, swap(here, step)], 0)
        arrived = swap(here, last - 1)
        share, parcel = early(layout, side, own, mate, here)
        arrived, parcel = lax.optimization_barrier((arrived, parcel))
        there = swap(jnp.concatenate([arrived, parcel], 0), last)
        share = middle(layout, here.shape[0], side, own, arrived, share)
        return finish(layout, side, own, there, share)

    in_specs = (P(None, ("blk", "grp")), P(None, ("blk", "grp")), P(), P(), P())
    out_specs = (P(None, ("blk", "grp")), P(None, ("blk", "grp")))
    return jax.shard_map(local, mesh=mesh, in_specs=in_specs, out_specs=out_specs, check_vma=False)
```
